256 devices in a mesh: dom: 32 (over x, y, core), board: 8 (over z).
Axes of the slice: x: 4, y: 4, z: 8, core: 2. Of those that a mesh axis runs over, the one named last changes fastest.
Arguments:
- block: bfloat16 [64, 1048576], P(None, ('dom', 'board')), may hold values from -120 to 120, as said below
- tiles: bfloat16 [8192, 10, 128, 128], P(('dom', 'board')), may hold values from -0.15625 to 0.15625
- cols: int32 [8192, 10], P(('dom', 'board')), may hold values from 0 to 8191, as said below
- counts: int32 [8192], P(('dom', 'board')), may hold values from 2 to 10, as said below
Outputs:
- basis: bfloat16 [64, 1048576], P(None, ('dom', 'board'))
- projected: float32 [64, 64], replicated
The draws below stay inside these ranges and needn't reach their ends.
Inputs may be any that keep to these rules, and one draw needn't show every extreme that they name: `block`: entries are below 120 in magnitude. `cols`: slot 0 of row r holds column r; slot 1 holds r + 8 or r - 8 (where that lies in the grid, else the nearest end); every column lies within 8 of its row. `counts`: slots at or past the count are ignored.
All inputs are finite; a program needn't handle non-finite values.
Results may differ from the reference program's by a relative error of at most 0.0072.
Values may be sent and summed in bfloat16 or wider, within the bound.
No kernel may reach another device: no remote copies, remote signals or barrier semaphores. Data moves between devices by JAX's collectives and lax.ppermute only.
A program may use at most 64 MiB of HBM per device.

```python
import math
import jax
import jax.numpy as jnp
from jax import lax

K = 64
TB = 128
SLOTS = 10
DEG = 4
TD = 32
GHOST = 8
NT = 8192
NODES = 1048576


def draw_block(key, part):
    key = jax.random.fold_in(key, 11)
    first_key, node_key, vector_key = jax.random.split(key, 3)
    node_scale = jnp.exp(jax.random.uniform(node_key, (1, NODES), minval=0.0, maxval=math.log(10.0)))
    ramp = jnp.exp(math.log(3.0) * jnp.arange(NODES, dtype=jnp.float32)[None, :] / NODES)
    vector_scale = jnp.exp(jax.random.uniform(vector_key, (K, 1), minval=0.0, maxval=math.log(10.0)))
    values = jax.random.normal(first_key, (K, NODES))
    values = jnp.clip(values, -4.0, 4.0)
    return (values * node_scale * ramp * vector_scale * 0.1).astype(jnp.bfloat16)


def draw_cols(key, part):
    key = jax.random.fold_in(key, 23)
    offset_key, sign_key = jax.random.split(key)
    rows = jnp.arange(NT, dtype=jnp.int32)[:, None]
    offsets = jax.random.randint(offset_key, (NT, SLOTS), -GHOST, GHOST + 1)
    signs = 2 * jax.random.randint(sign_key, (NT, 1), 0, 2) - 1
    slot = jnp.arange(SLOTS, dtype=jnp.int32)[None, :]
    offsets = jnp.where(slot == 0, 0, jnp.where(slot == 1, signs * GHOST, offsets))
    return jnp.clip(rows + offsets, 0, NT - 1).astype(jnp.int32)


def draw_counts(key, part):
    key = jax.random.fold_in(key, 37)
    level_key, raw_key, chosen_key = jax.random.split(key, 3)
    groups = NT // TD
    level = jax.random.randint(level_key, (groups, 1), 2, SLOTS + 1)
    raw = jax.random.randint(raw_key, (groups, TD), 0, 1 << 20)
    count = (2 + raw % (level - 1)).reshape(NT)
    chosen = jax.random.randint(chosen_key, (), 0, NT)
    return jnp.where(jnp.arange(NT, dtype=jnp.int32) == chosen, SLOTS, count).astype(jnp.int32)


def shard_levels(stream_key, extent, cuts, low, high):
    gain = 1.0
    for axis_at, parts in cuts:
        heights = jax.random.uniform(jax.random.fold_in(jax.random.fold_in(stream_key, 6), axis_at), (parts,), jnp.float32, low / len(cuts), high / len(cuts))
        gain = gain * jnp.repeat(jnp.exp(heights), extent[axis_at] // parts).reshape((-1,) + (1,) * (len(extent) - 1 - axis_at))
    return gain


def normal_values(rng, extent, width, reach, cuts=(), held_as=jnp.bfloat16):
    entries = width * jax.random.normal(rng, extent, jnp.float32)
    if cuts:
        entries = entries * shard_levels(rng, extent, cuts, -0.22, 0.18)
    return jnp.clip(entries, -reach, reach).astype(held_as)


def setup_inputs(seed: int = 0) -> dict:
    streams_of = jax.random.split(jax.random.key(seed), 5)
    return {
        "block": draw_block(jax.random.fold_in(streams_of[4], 71), 0),
        "tiles": normal_values(streams_of[1], (NT, SLOTS, TB, TB), (SLOTS * TB) ** -0.5, 0.15625, ((0, 256),)),
        "cols": draw_cols(jax.random.fold_in(streams_of[4], 71), 0),
        "counts": draw_counts(jax.random.fold_in(streams_of[4], 71), 0),
    }


def apply_all(field, tiles, cols, counts):
    rows_of = field.shape[0]
    blocks = field.astype(jnp.float32).reshape(rows_of, NT, TB)
    tile_rows = tiles.reshape(NT // TD, TD, SLOTS, TB, TB)
    col_rows = cols.reshape(NT // TD, TD, SLOTS)
    count_rows = counts.reshape(NT // TD, TD)

    def one_part(pieces):
        tile_part, col_part, count_part = pieces
        picked = jnp.take(blocks, col_part, axis=1)
        live = (lax.broadcasted_iota(jnp.int32, col_part.shape, 1) < count_part[:, None]).astype(jnp.float32)
        picked = picked * live[None, :, :, None]
        return jnp.einsum('krsj,rsij->kri', picked, tile_part.astype(jnp.float32))
    result = lax.map(one_part, (tile_rows, col_rows, count_rows))
    return jnp.transpose(result, (1, 0, 2, 3)).reshape(rows_of, NODES)

def reference(block, tiles, cols, counts):
    older = block
    current = block
    for degree in range(DEG):
        image = apply_all(current, tiles, cols, counts)
        if degree > 0:
            image = 2.0 * image - older.astype(jnp.float32)
        older, current = (current, image.astype(jnp.bfloat16))
    filtered = current
    image = apply_all(filtered, tiles, cols, counts).astype(jnp.bfloat16)
    gram = jnp.dot(filtered.astype(jnp.float32), filtered.T.astype(jnp.float32), preferred_element_type=jnp.float32) / NODES
    cross = jnp.dot(filtered.astype(jnp.float32), image.T.astype(jnp.float32), preferred_element_type=jnp.float32) / NODES
    factor = jnp.linalg.cholesky(gram)
    identity = jnp.eye(K, dtype=jnp.float32)
    inverse = jax.scipy.linalg.solve_triangular(factor, identity, lower=True)
    basis = jnp.dot(inverse, filtered.astype(jnp.float32), precision=lax.Precision.HIGHEST).astype(jnp.bfloat16)
    half = jnp.dot(inverse, cross, precision=lax.Precision.HIGHEST)
    projected = jnp.dot(half, inverse.T, precision=lax.Precision.HIGHEST)
    return (basis, projected)
```

```python
import functools

import jax
import jax.numpy as jnp
import numpy as np
from jax import lax
from jax.experimental import pallas as pl
from jax.experimental.pallas import tpu as pltpu
from jax.sharding import PartitionSpec as P

DEG = 4
GHOST = 8
TB = 128
AX = ("dom", "board")
MIB = 1 << 20
NT_DIMS = (((1,), (1,)), ((), ()))
UNROLL = 4

VM = pl.BlockSpec(memory_space=pltpu.VMEM)
SM = pl.BlockSpec(memory_space=pltpu.SMEM)
ANY = pl.BlockSpec(memory_space=pl.ANY)


def call(kernel, out_shape, in_specs, out_specs, scratch=(), limit=24, flops=0, bytes_=0):
    return pl.pallas_call(
        kernel,
        out_shape=out_shape,
        in_specs=in_specs,
        out_specs=out_specs,
        scratch_shapes=scratch,
        compiler_params=pltpu.CompilerParams(vmem_limit_bytes=limit * MIB),
        cost_estimate=pl.CostEstimate(flops=flops, bytes_accessed=bytes_, transcendentals=0),
    )


def pair_dot(src, tiles, row, pair, left, right):
    lhs = jnp.concatenate(
        [src[:, pl.ds(pl.multiple_of(left, TB), TB)], src[:, pl.ds(pl.multiple_of(right, TB), TB)]], axis=1
    )
    rhs = jnp.concatenate([tiles[row, 2 * pair], tiles[row, 2 * pair + 1]], axis=1)
    return lax.dot_general(lhs, rhs, NT_DIMS, preferred_element_type=jnp.float32)


def row_sum(src, tiles, tab, row):
    total = None
    for pair in range(5):
        term = pair_dot(src, tiles, row, pair, tab[row, 2 * pair], tab[row, 2 * pair + 1])
        total = term if total is None else total + term
    return total


def own_products(src, tiles, tab, acc):
    rows = tiles.shape[0]

    def step(g, carry):
        for u in range(UNROLL):
            row = g * UNROLL + u
            acc[:, pl.ds(pl.multiple_of(row * TB, TB), TB)] = row_sum(src, tiles, tab, row)
        return carry

    lax.fori_loop(0, rows // UNROLL, step, 0)


def load_kernel(block, tiles_hbm, tab, tiles, acc, src, sems):
    rows = tiles.shape[0]
    parts = sems.shape[0]
    each = rows // parts
    copies = [
        pltpu.make_async_copy(tiles_hbm.at[pl.ds(p * each, each)], tiles.at[pl.ds(p * each, each)], sems.at[p])
        for p in range(parts)
    ]
    for c in copies:
        c.start()
    wide = block.shape[1]
    src[:, :wide] = block[...]
    src[:, wide:] = jnp.zeros_like(src[:, wide:])
    for c in copies:
        c.wait()
    own_products(src, tiles, tab, acc)


def own_kernel(src, tiles, tab, acc):
    own_products(src, tiles, tab, acc)


def halo_products(acc, older, r0, r1, tiles, tab, par, out, halo):
    rows = tiles.shape[0]
    edge = GHOST * TB
    odd = par[0]

    @pl.when(odd == 1)
    def _():
        halo[:, :edge] = r0[...]
        halo[:, edge : 2 * edge] = r1[...]

    @pl.when(odd == 0)
    def _():
        halo[:, :edge] = r1[...]
        halo[:, edge : 2 * edge] = r0[...]

    halo[:, 2 * edge :] = jnp.zeros_like(halo[:, 2 * edge :])

    def finish(row, value):
        at = pl.ds(pl.multiple_of(row * TB, TB), TB)
        if older is not None:
            value = 2.0 * value - older[:, at].astype(jnp.float32)
        out[:, at] = value.astype(jnp.bfloat16)

    def step(g, carry):
        for u in range(UNROLL):
            k = g * UNROLL + u
            row = jnp.where(k < GHOST, k, k + rows - 2 * GHOST)
            at = pl.ds(pl.multiple_of(row * TB, TB), TB)
            finish(row, acc[:, at] + row_sum(halo, tiles, tab, row))
        return carry

    lax.fori_loop(0, 2 * GHOST // UNROLL, step, 0)
    for row in range(GHOST, rows - GHOST):
        finish(row, acc[:, row * TB : (row + 1) * TB])


def halo_kernel(acc, older, r0, r1, tiles, tab, par, out, s0, s1, halo, *, cheb):
    wide = tiles.shape[0] * TB
    edge = GHOST * TB
    odd = par[0]
    halo_products(acc, older if cheb else None, r0, r1, tiles, tab, par, out, halo)
    out[:, wide:] = jnp.zeros_like(out[:, wide:])

    @pl.when(odd == 1)
    def _():
        s0[...] = out[:, :edge]
        s1[...] = out[:, wide - edge : wide]

    @pl.when(odd == 0)
    def _():
        s0[...] = out[:, wide - edge : wide]
        s1[...] = out[:, :edge]


def last_kernel(acc, y, r0, r1, tiles, tab, par, both, halo, image):
    wide = image.shape[1]
    halo_products(acc, None, r0, r1, tiles, tab, par, image, halo)
    values = jnp.concatenate([y[:, :wide], image[...]], axis=0)
    both[...] = lax.dot_general(y[:, :wide], values, NT_DIMS, preferred_element_type=jnp.float32)


def eliminate(gram):
    size = gram.shape[0]
    lanes = lax.broadcasted_iota(jnp.int32, (size, 2 * size), 1)
    sublanes = lax.broadcasted_iota(jnp.int32, (size, 2 * size), 0)
    work = jnp.concatenate([gram, jnp.zeros_like(gram)], axis=1)
    work = jnp.where(lanes == sublanes + size, 1.0, work)
    for k in range(size):
        row = work[k : k + 1, :]
        pivot = work[k : k + 1, k : k + 1]
        scaled = row * lax.rsqrt(pivot)
        factor = work[:, k : k + 1] / pivot
        rest = work - factor * row
        work = jnp.where(sublanes == k, scaled, jnp.where(sublanes > k, rest, work))
    return work[:, size:]


def split3(x):
    hi = x.astype(jnp.bfloat16)
    rest = x - hi.astype(jnp.float32)
    mid = rest.astype(jnp.bfloat16)
    low = (rest - mid.astype(jnp.float32)).astype(jnp.bfloat16)
    return hi, mid, low


def end_kernel(both, y, basis, projected, *, nodes_all):
    size = both.shape[0]
    values = both[...] / nodes_all
    inverse = eliminate(values[:, :size])
    cross = values[:, size:]
    half = jnp.dot(inverse, cross, precision=lax.Precision.HIGHEST, preferred_element_type=jnp.float32)
    projected[...] = lax.dot_general(
        half, inverse, NT_DIMS, precision=lax.Precision.HIGHEST, preferred_element_type=jnp.float32
    )
    parts = jnp.concatenate(split3(inverse), axis=0)
    chunk = 512

    def step(c, carry):
        at = pl.ds(pl.multiple_of(c * chunk, chunk), chunk)
        out = jnp.dot(parts, y[:, at], preferred_element_type=jnp.float32)
        basis[:, at] = (out[:size] + (out[size : 2 * size] + out[2 * size :])).astype(jnp.bfloat16)
        return carry

    lax.fori_loop(0, basis.shape[1] // chunk, step, 0)


def rotations(shape, axis):
    at = np.arange(int(np.prod(shape))).reshape(shape)
    return [
        list(zip(at.reshape(-1).tolist(), np.roll(at, -k, axis=axis).reshape(-1).tolist()))
        for k in range(1, shape[axis])
    ]


def all_sum(x, dom, board):
    shape = (dom // 8, 4, 2, board) if dom % 8 == 0 else (dom, 1, 1, board)
    for axis in (2, 1, 0, 3):
        pieces = [lax.ppermute(x, AX, perm) for perm in rotations(shape, axis)]
        for piece in pieces:
            x = x + piece
    return x


def body(block, tiles, cols, counts, *, dom, board):
    devices = dom * board
    size, wide = block.shape
    rows, slots = cols.shape
    edge = GHOST * TB
    padded = wide + TB
    bf16, f32 = jnp.bfloat16, jnp.float32
    shape = jax.ShapeDtypeStruct
    me = lax.axis_index(AX)
    first = me * rows
    odd = me % 2
    par = odd.reshape(1).astype(jnp.int32)

    even_pairs = [(i, i ^ 1) for i in range(devices)]
    odd_pairs = [(0, 0), (devices - 1, devices - 1)] + [(i, ((i + 1) ^ 1) - 1) for i in range(1, devices - 1)]

    def exchange(s0, s1):
        r1 = lax.ppermute(s1, AX, odd_pairs)
        r0 = lax.ppermute(s0, AX, even_pairs)
        return r0, r1

    live = lax.broadcasted_iota(jnp.int32, cols.shape, 1) < counts[:, None]
    near = cols - first
    inside = (near >= 0) & (near < rows)
    tab_own = jnp.where(live & inside, near, rows) * TB
    beyond = jnp.where(near < 0, near + GHOST, near - rows + GHOST)
    tab_halo = jnp.where(live & ~inside, beyond, 2 * GHOST) * TB

    head, tail = block[:, :edge], block[:, wide - edge :]
    r0, r1 = exchange(jnp.where(odd == 1, head, tail), jnp.where(odd == 1, tail, head))

    pair_flops = 2 * size * TB * TB
    own_flops = rows * slots * pair_flops
    halo_flops = own_flops // 2
    tile_bytes = tiles.size * 2
    acc_shape = shape((size, wide), f32)
    y_shape = shape((size, padded), bf16)
    edge_shape = shape((size, edge), bf16)
    halo_scratch = pltpu.VMEM((size, 2 * edge + TB), bf16)

    tiles_v, acc = call(
        load_kernel,
        [pltpu.VMEM(tiles.shape, bf16), acc_shape],
        [VM, ANY, SM],
        [VM, VM],
        [pltpu.VMEM((size, padded), bf16), pltpu.SemaphoreType.DMA((4,))],
        flops=own_flops,
        bytes_=tile_bytes,
    )(block, tiles, tab_own)

    older, y = block, block
    for degree in range(DEG):
        new, s0, s1 = call(
            functools.partial(halo_kernel, cheb=degree > 0),
            [y_shape, edge_shape, edge_shape],
            [VM, VM, VM, VM, VM, SM, SM],
            [VM, VM, VM],
            [halo_scratch],
            flops=halo_flops,
        )(acc, older, r0, r1, tiles_v, tab_halo, par)
        older, y = y, new
        r0, r1 = exchange(s0, s1)
        acc = call(own_kernel, acc_shape, [VM, VM, SM], VM, flops=own_flops)(y, tiles_v, tab_own)

    both = call(
        last_kernel,
        shape((size, 2 * size), f32),
        [VM, VM, VM, VM, VM, SM, SM],
        VM,
        [halo_scratch, pltpu.VMEM((size, wide), bf16)],
        flops=halo_flops,
    )(acc, y, r0, r1, tiles_v, tab_halo, par)
    both = all_sum(both, dom, board)
    basis, projected = call(
        functools.partial(end_kernel, nodes_all=devices * rows * TB),
        [shape((size, wide), bf16), shape((size, size), f32)],
        [VM, VM],
        [VM, VM],
        flops=6 * size * size * wide,
    )(both, y)
    return basis, projected


def solution(mesh):
    dom, board = mesh.shape["dom"], mesh.shape["board"]
    return jax.shard_map(
        functools.partial(body, dom=dom, board=board),
        mesh=mesh,
        in_specs=(
            P(None, AX),
            P(AX, None, None, None),
            P(AX, None),
            P(AX),
        ),
        out_specs=(P(None, AX), P()),
        check_vma=False,
    )
```

```python
import functools

import jax
import jax.numpy as jnp
import numpy as np
from jax import lax
from jax.experimental import pallas as pl
from jax.experimental.pallas import tpu as pltpu
from jax.sharding import PartitionSpec as P

DEG = 4
GHOST = 8
TB = 128
AX = ("dom", "board")
MIB = 1 << 20
NN_DIMS = (((1,), (0,)), ((), ()))
NT_DIMS = (((1,), (1,)), ((), ()))
GROUP = 8
SMALL = 4

VM = pl.BlockSpec(memory_space=pltpu.VMEM)
SM = pl.BlockSpec(memory_space=pltpu.SMEM)
HBM = pl.BlockSpec(memory_space=pltpu.HBM)

OWN, SLOT, BLOCK, NEED, MISC = 0, 10, 20, 30, 31
TABLE = (32, 128)


def call(kernel, out_shape, in_specs, out_specs, scratch=(), limit=24, flops=0, bytes_=0):
    return pl.pallas_call(
        kernel,
        out_shape=out_shape,
        in_specs=in_specs,
        out_specs=out_specs,
        scratch_shapes=scratch,
        compiler_params=pltpu.CompilerParams(vmem_limit_bytes=limit * MIB),
        cost_estimate=pl.CostEstimate(flops=flops, bytes_accessed=bytes_, transcendentals=0),
    )


def stay(x):
    return pltpu.with_memory_space_constraint(x, pltpu.HBM)


def block_at(ref, offset):
    return ref[:, pl.ds(pl.multiple_of(offset, TB), TB)]


def own_row(src, tiles, tab, row, slots):
    total = None
    for pair in range(slots // 2):
        lhs = jnp.concatenate(
            [block_at(src, tab[OWN + 2 * pair, row]), block_at(src, tab[OWN + 2 * pair + 1, row])], axis=1
        )
        rhs = tiles(row, pair)
        term = lax.dot_general(lhs, rhs, NN_DIMS, preferred_element_type=jnp.float32)
        total = term if total is None else total + term
    return total


def gather_field(src, s0, mid, s1):
    edge, inner = s0.shape[1], mid.shape[1]
    src[:, :edge] = s0[...]
    src[:, edge : edge + inner] = mid[...]
    src[:, edge + inner : 2 * edge + inner] = s1[...]
    src[:, 2 * edge + inner :] = jnp.zeros_like(src[:, 2 * edge + inner :])


def own_products(src, pair_of, tab, old, acc, new, cheb, slots, rows, before=None, group=GROUP):
    def place(u, value):
        at = pl.ds(pl.multiple_of(u * TB, TB), TB)
        if cheb:
            value = 2.0 * value - old[:, at].astype(jnp.float32)
        new[:, at] = value.astype(jnp.bfloat16)

    def side(u, value):
        acc[:, pl.ds(pl.multiple_of(u * TB, TB), TB)] = value

    def sweep(first, out, count, store):
        def step(g, carry):
            if before is not None:
                before(first + g * group)
            values = [own_row(src, pair_of, tab, first + g * group + u, slots) for u in range(group)]
            for u in range(group):
                store(out + g * group + u, values[u])
            return carry

        lax.fori_loop(0, count // group, step, 0)

    lead, trail = tab[MISC, 0], tab[MISC, 1]
    sweep(lead, 0, GHOST, side)
    sweep(GHOST, 0, rows - 2 * GHOST, place)
    sweep(trail, GHOST, GHOST, side)


def held_pairs(tiles):
    return lambda row, pair: tiles[row, 2 * pair * TB : 2 * (pair + 1) * TB, :]


def fill_table(cols, counts, place, lines, rows, slots):
    first, odd, core = place[0], place[1], place[2]
    lead = (1 - odd) * (rows - GHOST)
    near = cols[...] - first
    live = lax.broadcasted_iota(jnp.int32, near.shape, 0) < counts[...]
    inside = (near >= 0) & (near < rows)
    spot = jnp.where(near < GHOST, near + lead, jnp.where(near >= rows - GHOST, near - lead, near))
    lines[OWN : OWN + slots, :rows] = jnp.where(live & inside, spot, rows) * TB
    out = jnp.where(live & ~inside, 1, 0)
    there = jnp.where(near < 0, near + GHOST + GHOST * (1 - odd), near - rows + GHOST * odd) * TB
    empty = jnp.zeros((1, rows), jnp.int32)
    found = empty
    slot_lines, block_lines = [empty] * slots, [empty + 2 * GHOST * TB] * slots
    for s in range(slots):
        here = out[s : s + 1]
        for q in range(s + 1):
            hit = (here == 1) & (found == q)
            slot_lines[q] = jnp.where(hit, s * TB, slot_lines[q])
            block_lines[q] = jnp.where(hit, there[s : s + 1], block_lines[q])
        found = found + here
    for q in range(slots):
        lines[SLOT + q : SLOT + q + 1, :rows] = slot_lines[q]
        lines[BLOCK + q : BLOCK + q + 1, :rows] = block_lines[q]
    lines[NEED : NEED + 1, :rows] = found
    lane = lax.broadcasted_iota(jnp.int32, (1, rows), 1)
    lines[MISC : MISC + 1, :rows] = jnp.where(lane == 0, lead, jnp.where(lane == 1, rows - GHOST - lead, core))


def load_kernel(
    s0, s1, block, tiles_hbm, cols_hbm, counts_hbm, place, tiles, acc, mid0, new, tab, src, raw, cols, counts, lines,
    sems, small_sems,
):
    rows, slots = raw.shape[0], raw.shape[1]
    edge = GHOST * TB
    chunk = GROUP
    little = [
        pltpu.make_async_copy(cols_hbm, cols, small_sems.at[0]),
        pltpu.make_async_copy(counts_hbm, counts, small_sems.at[1]),
        pltpu.make_async_copy(block.at[:, pl.ds(edge, mid0.shape[1])], mid0, small_sems.at[2]),
    ]
    for copy in little:
        copy.start()

    def piece(start):
        return pltpu.make_async_copy(
            tiles_hbm.at[pl.ds(start, chunk)], raw.at[pl.ds(start, chunk)], sems.at[lax.div(start, chunk)]
        )

    lead = (1 - place[1]) * (rows - GHOST)
    for c in range(GHOST // chunk):
        piece(lead + c * chunk).start()
    for c in range(GHOST // chunk, (rows - GHOST) // chunk):
        piece(c * chunk).start()
    for c in range(GHOST // chunk):
        piece(rows - GHOST - lead + c * chunk).start()
    little[0].wait()
    little[1].wait()
    fill_table(cols, counts, place, lines, rows, slots)
    to_scalars = pltpu.make_async_copy(lines, tab, small_sems.at[3])
    to_scalars.start()
    little[2].wait()
    gather_field(src, s0, mid0, s1)
    to_scalars.wait()

    def pair_of(row, pair):
        turned = jnp.concatenate([raw[row, 2 * pair].T, raw[row, 2 * pair + 1].T], axis=0)
        tiles[row, 2 * pair * TB : 2 * (pair + 1) * TB, :] = turned
        return turned

    own_products(
        src, pair_of, tab, None, acc, new, False, slots, rows, before=lambda start: piece(start).wait(), group=chunk
    )


def own_kernel(s0, mid, s1, old, tiles, tab, acc, new, src, *, slots):
    gather_field(src, s0, mid, s1)
    own_products(src, held_pairs(tiles), tab, old, acc, new, True, slots, tiles.shape[0])


def own_last_kernel(s0, mid, s1, tiles, tab, acc, both, src, new, *, slots):
    gather_field(src, s0, mid, s1)
    own_products(src, held_pairs(tiles), tab, None, acc, new, False, slots, tiles.shape[0])
    edge, inner = s0.shape[1], mid.shape[1]
    size = mid.shape[0]
    mids = mid[...]
    total = lax.dot_general(
        mids, jnp.concatenate([mids, new[...]], axis=0), NT_DIMS, preferred_element_type=jnp.float32
    )
    gram = jnp.zeros((size, size), jnp.float32)
    for side in (s0[...], s1[...]):
        gram = gram + lax.dot_general(side, side, NT_DIMS, preferred_element_type=jnp.float32)
    both[...] = total + jnp.concatenate([gram, jnp.zeros_like(gram)], axis=1)


def halo_products(acc, r0, r1, tiles, tab, halo, sums, slots):
    edge = GHOST * TB
    halo[:, :edge] = r0[...]
    halo[:, edge : 2 * edge] = r1[...]
    halo[:, 2 * edge :] = jnp.zeros_like(halo[:, 2 * edge :])

    first = (tab[MISC, 0], tab[MISC, 1])

    def term(k, pair):
        row = first[k // GHOST] + k % GHOST
        lhs = jnp.concatenate(
            [block_at(halo, tab[BLOCK + 2 * pair, row]), block_at(halo, tab[BLOCK + 2 * pair + 1, row])], axis=1
        )
        rhs = jnp.concatenate(
            [tiles[row, pl.ds(pl.multiple_of(tab[SLOT + 2 * pair + e, row], TB), TB), :] for e in (0, 1)], axis=0
        )
        return lax.dot_general(lhs, rhs, NN_DIMS, preferred_element_type=jnp.float32)

    for half in (0, GHOST):
        terms = [term(half + u, 0) for u in range(GHOST)]
        for u in range(GHOST):
            at = slice((half + u) * TB, (half + u + 1) * TB)
            sums[:, at] = acc[:, at] + terms[u]
    for g in range(2 * GHOST // SMALL):
        start = first[g * SMALL // GHOST] + g * SMALL % GHOST
        need = tab[NEED, start]
        for u in range(1, SMALL):
            need = jnp.maximum(need, tab[NEED, start + u])

        def more(pair, carry, g=g):
            terms = [term(g * SMALL + u, pair) for u in range(SMALL)]
            for u in range(SMALL):
                at = slice((g * SMALL + u) * TB, (g * SMALL + u + 1) * TB)
                sums[:, at] += terms[u]
            return carry

        lax.fori_loop(1, lax.div(need + 1, 2), more, 0)


def halo_kernel(acc, old0, old1, r0, r1, tiles, tab, s0, s1, halo, sums, *, cheb, slots):
    edge = GHOST * TB
    halo_products(acc, r0, r1, tiles, tab, halo, sums, slots)
    for side, old, new in ((0, old0, s0), (1, old1, s1)):
        value = sums[:, side * edge : (side + 1) * edge]
        if cheb:
            value = 2.0 * value - old[...].astype(jnp.float32)
        new[...] = value.astype(jnp.bfloat16)


def halo_last_kernel(acc, s0, s1, r0, r1, tiles, tab, both, keep, give, whole, halo, sums, *, slots):
    edge = GHOST * TB
    size = both.shape[0]
    halo_products(acc, r0, r1, tiles, tab, halo, sums, slots)
    cross = both[:, size:]
    for side, y in ((0, s0), (1, s1)):
        image = sums[:, side * edge : (side + 1) * edge].astype(jnp.bfloat16)
        cross = cross + lax.dot_general(y[...], image, NT_DIMS, preferred_element_type=jnp.float32)
    whole[...] = jnp.concatenate([both[:, :size], cross], axis=1)
    half = size // 2
    mine = pl.multiple_of(tab[MISC, 2] * half, half)
    keep[...] = whole[pl.ds(mine, half), :]
    give[...] = whole[pl.ds(pl.multiple_of(half - mine, half), half), :]


def eliminate(gram):
    size = gram.shape[0]
    step, sub = 4, 8
    lanes = lax.broadcasted_iota(jnp.int32, (sub, 2 * size), 1)
    inner = lax.broadcasted_iota(jnp.int32, (sub, 2 * size), 0)
    wide = jnp.concatenate([gram, jnp.zeros_like(gram)], axis=1)
    work = [
        jnp.where(lanes == inner + g * sub + size, 1.0, wide[g * sub : (g + 1) * sub]) for g in range(size // sub)
    ]
    for k in range(0, size, step):
        g0, off = divmod(k, sub)
        cols = [
            {g: jnp.broadcast_to(work[g][:, k + j : k + j + 1], (sub, 2 * size)) for g in range(g0, size // sub)}
            for j in range(step)
        ]
        rows = [work[g0][off + j : off + j + 1] for j in range(step)]
        units = []
        finals = []
        for j in range(step):
            pivot = cols[j][g0][off + j : off + j + 1]
            inverse = 1.0 / pivot
            unit = rows[j] * inverse
            units.append(unit)
            finals.append(rows[j] * lax.rsqrt(pivot))
            for m in range(j + 1, step):
                rows[m] = rows[m] - cols[j][g0][off + m : off + m + 1] * unit
                factor = cols[m][g0][off + j : off + j + 1] * inverse
                cols[m] = {g: cols[m][g] - cols[j][g] * factor for g in cols[m]}
        for g in range(g0, size // sub):
            value = work[g]
            for j in range(step):
                value = value - cols[j][g] * units[j]
            if g == g0:
                value = jnp.where(inner >= off + step, value, work[g])
                for j in range(step):
                    value = jnp.where(inner == off + j, finals[j], value)
            work[g] = value
    return jnp.concatenate(work, axis=0)[:, size:]


def split3(x):
    hi = x.astype(jnp.bfloat16)
    rest = x - hi.astype(jnp.float32)
    mid = rest.astype(jnp.bfloat16)
    low = (rest - mid.astype(jnp.float32)).astype(jnp.bfloat16)
    return hi, mid, low


def end_kernel(mine, other, s0, mid, s1, tab, basis, projected, both, *, nodes_all):
    size = both.shape[0]
    half = size // 2
    at = pl.multiple_of(tab[MISC, 2] * half, half)
    both[pl.ds(at, half), :] = mine[...]
    both[pl.ds(pl.multiple_of(half - at, half), half), :] = other[...]
    edge, inner = s0.shape[1], mid.shape[1]
    values = both[...] / nodes_all
    inverse = eliminate(values[:, :size])
    cross = values[:, size:]
    parts = jnp.concatenate(split3(inverse), axis=0)

    def piece(y):
        out = jnp.dot(parts, y, preferred_element_type=jnp.float32)
        return (out[:size] + (out[size : 2 * size] + out[2 * size :])).astype(jnp.bfloat16)

    lead = pl.multiple_of(tab[MISC, 0] * TB, TB)
    trail = pl.multiple_of(tab[MISC, 1] * TB, TB)
    basis[:, pl.ds(lead, edge)] = piece(s0[...])
    basis[:, pl.ds(trail, edge)] = piece(s1[...])
    for c in range(0, inner, edge):
        basis[:, edge + c : 2 * edge + c] = piece(mid[:, c : c + edge])
    half = jnp.dot(inverse, cross, precision=lax.Precision.HIGHEST, preferred_element_type=jnp.float32)
    projected[...] = lax.dot_general(
        half, inverse, NT_DIMS, precision=lax.Precision.HIGHEST, preferred_element_type=jnp.float32
    )


def rotations(shape, axis):
    at = np.arange(int(np.prod(shape))).reshape(shape)
    return [
        list(zip(at.reshape(-1).tolist(), np.roll(at, -k, axis=axis).reshape(-1).tolist()))
        for k in range(1, shape[axis])
    ]


def all_sum(keep, give, dom, board):
    shape = (dom // 8, 4, 2, board)
    (swap,) = rotations(shape, 2)
    x = keep + lax.ppermute(give, AX, swap)
    planes = np.arange(dom * board).reshape(-1, 2 * board).T.tolist()
    spread = jnp.broadcast_to(x[None], (dom // 2,) + x.shape)
    x = lax.all_to_all(spread, AX, 0, 0, axis_index_groups=planes).sum(0)
    spread = jnp.broadcast_to(x[None], (board,) + x.shape)
    x = lax.all_to_all(spread, "board", 0, 0).sum(0)
    return x, lax.ppermute(x, AX, swap)


def body(block, tiles, cols, counts, *, dom, board):
    devices = dom * board
    size, wide = block.shape
    rows, slots = cols.shape
    edge = GHOST * TB
    inner = wide - 2 * edge
    bf16, f32 = jnp.bfloat16, jnp.float32
    shape = jax.ShapeDtypeStruct
    me = lax.axis_index(AX)
    odd = me % 2
    core = (me // board) % 2
    place = jnp.stack([me * rows, odd, core]).astype(jnp.int32)

    even_pairs = [(i, i ^ 1) for i in range(devices)]
    odd_pairs = [(i, (((i + 1) ^ 1) - 1) % devices) for i in range(devices)]

    def exchange(s0, s1):
        return lax.ppermute(s0, AX, even_pairs), lax.ppermute(s1, AX, odd_pairs)

    head, tail = block[:, :edge], block[:, wide - edge :]
    s0, s1 = jnp.where(odd == 1, head, tail), jnp.where(odd == 1, tail, head)
    r0, r1 = exchange(s0, s1)

    own_flops = 2 * rows * slots * size * TB * TB
    halo_flops = own_flops // 8
    acc_shape = shape((size, 2 * edge), f32)
    mid_shape = shape((size, inner), bf16)
    edge_shape = shape((size, edge), bf16)
    field = pltpu.VMEM((size, wide + TB), bf16)
    halo_scratch = [pltpu.VMEM((size, 2 * edge + TB), bf16), pltpu.VMEM((size, 2 * edge), f32)]

    tiles_v, acc, mid, new, tab = call(
        load_kernel,
        [shape((rows, slots * TB, TB), bf16), acc_shape, mid_shape, mid_shape, pltpu.SMEM(TABLE, jnp.int32)],
        [VM, VM, HBM, HBM, HBM, HBM, SM],
        [VM, VM, VM, VM, SM],
        [
            field,
            pltpu.VMEM(tiles.shape, bf16),
            pltpu.VMEM((slots, rows), jnp.int32),
            pltpu.VMEM((1, rows), jnp.int32),
            pltpu.VMEM(TABLE, jnp.int32),
            pltpu.SemaphoreType.DMA((rows // GROUP,)),
            pltpu.SemaphoreType.DMA((4,)),
        ],
        limit=40,
        flops=own_flops,
        bytes_=tiles.size * 2,
    )(s0, s1, *(stay(v) for v in (block, tiles, cols.T, counts.reshape(1, rows))), place)

    tab = pltpu.with_memory_space_constraint(tab, pltpu.SMEM)
    older = (s0, mid, s1)
    for degree in range(DEG):
        old0, old_mid, old1 = older
        older = (s0, mid, s1)
        s0, s1 = call(
            functools.partial(halo_kernel, cheb=degree > 0, slots=slots),
            [edge_shape, edge_shape],
            [VM, VM, VM, VM, VM, VM, SM],
            [VM, VM],
            halo_scratch,
            flops=halo_flops,
        )(acc, old0, old1, r0, r1, tiles_v, tab)
        mid = new
        r0, r1 = exchange(s0, s1)
        if degree < DEG - 1:
            acc, new = call(
                functools.partial(own_kernel, slots=slots),
                [acc_shape, mid_shape],
                [VM, VM, VM, VM, VM, SM],
                [VM, VM],
                [field],
                flops=own_flops,
            )(s0, mid, s1, older[1], tiles_v, tab)
        else:
            acc, both = call(
                functools.partial(own_last_kernel, slots=slots),
                [acc_shape, shape((size, 2 * size), f32)],
                [VM, VM, VM, VM, SM],
                [VM, VM],
                [field, pltpu.VMEM((size, inner), bf16)],
                flops=own_flops,
            )(s0, mid, s1, tiles_v, tab)

    half_shape = shape((size // 2, 2 * size), f32)
    keep, give = call(
        functools.partial(halo_last_kernel, slots=slots),
        [half_shape, half_shape],
        [VM, VM, VM, VM, VM, VM, SM, VM],
        [VM, VM],
        [pltpu.VMEM((size, 2 * size), f32)] + halo_scratch,
        flops=halo_flops,
    )(acc, s0, s1, r0, r1, tiles_v, tab, both)
    mine, other = all_sum(keep, give, dom, board)
    basis, projected = call(
        functools.partial(end_kernel, nodes_all=devices * rows * TB),
        [shape((size, wide), bf16), shape((size, size), f32)],
        [VM, VM, VM, VM, VM, SM],
        [VM, VM],
        [pltpu.VMEM((size, 2 * size), f32)],
        flops=6 * size * size * wide,
    )(mine, other, s0, mid, s1, tab)
    return basis, projected


def solution(mesh):
    dom, board = mesh.shape["dom"], mesh.shape["board"]
    return jax.shard_map(
        functools.partial(body, dom=dom, board=board),
        mesh=mesh,
        in_specs=(
            P(None, AX),
            P(AX, None, None, None),
            P(AX, None),
            P(AX),
        ),
        out_specs=(P(None, AX), P()),
        check_vma=False,
    )
```

```python
import functools

import jax
import jax.numpy as jnp
import numpy as np
from jax import lax
from jax.experimental import pallas as pl
from jax.experimental.pallas import tpu as pltpu
from jax.sharding import PartitionSpec as P

DEG = 4
GHOST = 8
TB = 128
AX = ("dom", "board")
MIB = 1 << 20
NN_DIMS = (((1,), (0,)), ((), ()))
NT_DIMS = (((1,), (1,)), ((), ()))
GROUP = 8
SMALL = 4

VM = pl.BlockSpec(memory_space=pltpu.VMEM)
SM = pl.BlockSpec(memory_space=pltpu.SMEM)
HBM = pl.BlockSpec(memory_space=pltpu.HBM)

OWN, SLOT, BLOCK, NEED, MISC = 0, 10, 20, 30, 31
TABLE = (32, 128)


def call(kernel, out_shape, in_specs, out_specs, scratch=(), limit=24, flops=0, bytes_=0):
    return pl.pallas_call(
        kernel,
        out_shape=out_shape,
        in_specs=in_specs,
        out_specs=out_specs,
        scratch_shapes=scratch,
        compiler_params=pltpu.CompilerParams(vmem_limit_bytes=limit * MIB),
        cost_estimate=pl.CostEstimate(flops=flops, bytes_accessed=bytes_, transcendentals=0),
    )


def stay(x):
    return pltpu.with_memory_space_constraint(x, pltpu.HBM)


def block_at(ref, offset):
    return ref[:, pl.ds(pl.multiple_of(offset, TB), TB)]


def own_row(src, tiles, tab, row, slots):
    total = None
    for pair in range(slots // 2):
        lhs = jnp.concatenate(
            [block_at(src, tab[OWN + 2 * pair, row]), block_at(src, tab[OWN + 2 * pair + 1, row])], axis=1
        )
        rhs = tiles(row, pair)
        term = lax.dot_general(lhs, rhs, NN_DIMS, preferred_element_type=jnp.float32)
        total = term if total is None else total + term
    return total


def gather_field(src, s0, mid, s1):
    edge, inner = s0.shape[1], mid.shape[1]
    src[:, :edge] = s0[...]
    src[:, edge : edge + inner] = mid[...]
    src[:, edge + inner : 2 * edge + inner] = s1[...]
    src[:, 2 * edge + inner :] = jnp.zeros_like(src[:, 2 * edge + inner :])


def own_products(src, pair_of, tab, old, acc, new, cheb, slots, rows, before=None, group=GROUP):
    def place(u, value):
        at = pl.ds(pl.multiple_of(u * TB, TB), TB)
        if cheb:
            value = 2.0 * value - old[:, at].astype(jnp.float32)
        new[:, at] = value.astype(jnp.bfloat16)

    def side(u, value):
        acc[:, pl.ds(pl.multiple_of(u * TB, TB), TB)] = value

    def sweep(first, out, count, store):
        def step(g, carry):
            if before is not None:
                before(first + g * group)
            values = [own_row(src, pair_of, tab, first + g * group + u, slots) for u in range(group)]
            for u in range(group):
                store(out + g * group + u, values[u])
            return carry

        lax.fori_loop(0, count // group, step, 0)

    lead, trail = tab[MISC, 0], tab[MISC, 1]
    sweep(lead, 0, GHOST, side)
    sweep(GHOST, 0, rows - 2 * GHOST, place)
    sweep(trail, GHOST, GHOST, side)


def held_pairs(tiles):
    return lambda row, pair: tiles[row, 2 * pair * TB : 2 * (pair + 1) * TB, :]


def fill_table(cols, counts, place, lines, rows, slots):
    first, odd, core = place[0], place[1], place[2]
    lead = (1 - odd) * (rows - GHOST)
    near = cols[...] - first
    live = lax.broadcasted_iota(jnp.int32, near.shape, 0) < counts[...]
    inside = (near >= 0) & (near < rows)
    spot = jnp.where(near < GHOST, near + lead, jnp.where(near >= rows - GHOST, near - lead, near))
    lines[OWN : OWN + slots, :rows] = jnp.where(live & inside, spot, rows) * TB
    out = jnp.where(live & ~inside, 1, 0)
    there = jnp.where(near < 0, near + GHOST + GHOST * (1 - odd), near - rows + GHOST * odd) * TB
    empty = jnp.zeros((1, rows), jnp.int32)
    found = empty
    slot_lines, block_lines = [empty] * slots, [empty + 2 * GHOST * TB] * slots
    for s in range(slots):
        here = out[s : s + 1]
        for q in range(s + 1):
            hit = (here == 1) & (found == q)
            slot_lines[q] = jnp.where(hit, s * TB, slot_lines[q])
            block_lines[q] = jnp.where(hit, there[s : s + 1], block_lines[q])
        found = found + here
    for q in range(slots):
        lines[SLOT + q : SLOT + q + 1, :rows] = slot_lines[q]
        lines[BLOCK + q : BLOCK + q + 1, :rows] = block_lines[q]
    lines[NEED : NEED + 1, :rows] = found
    lane = lax.broadcasted_iota(jnp.int32, (1, rows), 1)
    lines[MISC : MISC + 1, :rows] = jnp.where(lane == 0, lead, jnp.where(lane == 1, rows - GHOST - lead, core))


def load_kernel(
    s0, s1, block, tiles_hbm, cols_hbm, counts_hbm, tiles, acc, mid0, new, tab, src, raw, cols, counts, lines,
    sems, small_sems, *, board,
):
    rows, slots = raw.shape[0], raw.shape[1]
    edge = GHOST * TB
    chunk = GROUP
    me = lax.axis_index(AX)
    place = (me * rows, lax.rem(me, 2), lax.rem(lax.div(me, board), 2))
    little = [
        pltpu.make_async_copy(cols_hbm, cols, small_sems.at[0]),
        pltpu.make_async_copy(counts_hbm, counts, small_sems.at[1]),
        pltpu.make_async_copy(block.at[:, pl.ds(edge, mid0.shape[1])], mid0, small_sems.at[2]),
    ]
    for copy in little:
        copy.start()

    def piece(start):
        return pltpu.make_async_copy(
            tiles_hbm.at[pl.ds(start, chunk)], raw.at[pl.ds(start, chunk)], sems.at[lax.div(start, chunk)]
        )

    lead = (1 - place[1]) * (rows - GHOST)
    for c in range(GHOST // chunk):
        piece(lead + c * chunk).start()
    for c in range(GHOST // chunk, (rows - GHOST) // chunk):
        piece(c * chunk).start()
    for c in range(GHOST // chunk):
        piece(rows - GHOST - lead + c * chunk).start()
    little[0].wait()
    little[1].wait()
    fill_table(cols, counts, place, lines, rows, slots)
    to_scalars = pltpu.make_async_copy(lines, tab, small_sems.at[3])
    to_scalars.start()
    little[2].wait()
    gather_field(src, s0, mid0, s1)
    to_scalars.wait()

    def pair_of(row, pair):
        turned = jnp.concatenate([raw[row, 2 * pair].T, raw[row, 2 * pair + 1].T], axis=0)
        tiles[row, 2 * pair * TB : 2 * (pair + 1) * TB, :] = turned
        return turned

    own_products(
        src, pair_of, tab, None, acc, new, False, slots, rows, before=lambda start: piece(start).wait(), group=chunk
    )


def own_kernel(s0, mid, s1, old, tiles, tab, acc, new, src, *, slots):
    gather_field(src, s0, mid, s1)
    own_products(src, held_pairs(tiles), tab, old, acc, new, True, slots, tiles.shape[0])


def own_last_kernel(s0, mid, s1, tiles, tab, acc, both, src, new, *, slots):
    gather_field(src, s0, mid, s1)
    own_products(src, held_pairs(tiles), tab, None, acc, new, False, slots, tiles.shape[0])
    edge, inner = s0.shape[1], mid.shape[1]
    size = mid.shape[0]
    mids = mid[...]
    total = lax.dot_general(
        mids, jnp.concatenate([mids, new[...]], axis=0), NT_DIMS, preferred_element_type=jnp.float32
    )
    gram = jnp.zeros((size, size), jnp.float32)
    for side in (s0[...], s1[...]):
        gram = gram + lax.dot_general(side, side, NT_DIMS, preferred_element_type=jnp.float32)
    both[...] = total + jnp.concatenate([gram, jnp.zeros_like(gram)], axis=1)


def halo_products(acc, r0, r1, tiles, tab, halo, sums, slots):
    edge = GHOST * TB
    halo[:, :edge] = r0[...]
    halo[:, edge : 2 * edge] = r1[...]
    halo[:, 2 * edge :] = jnp.zeros_like(halo[:, 2 * edge :])

    first = (tab[MISC, 0], tab[MISC, 1])

    def term(k, pair):
        row = first[k // GHOST] + k % GHOST
        lhs = jnp.concatenate(
            [block_at(halo, tab[BLOCK + 2 * pair, row]), block_at(halo, tab[BLOCK + 2 * pair + 1, row])], axis=1
        )
        rhs = jnp.concatenate(
            [tiles[row, pl.ds(pl.multiple_of(tab[SLOT + 2 * pair + e, row], TB), TB), :] for e in (0, 1)], axis=0
        )
        return lax.dot_general(lhs, rhs, NN_DIMS, preferred_element_type=jnp.float32)

    for half in (0, GHOST):
        terms = [term(half + u, 0) for u in range(GHOST)]
        for u in range(GHOST):
            at = slice((half + u) * TB, (half + u + 1) * TB)
            sums[:, at] = acc[:, at] + terms[u]
    for g in range(2 * GHOST // SMALL):
        start = first[g * SMALL // GHOST] + g * SMALL % GHOST
        need = tab[NEED, start]
        for u in range(1, SMALL):
            need = jnp.maximum(need, tab[NEED, start + u])

        def more(pair, carry, g=g):
            terms = [term(g * SMALL + u, pair) for u in range(SMALL)]
            for u in range(SMALL):
                at = slice((g * SMALL + u) * TB, (g * SMALL + u + 1) * TB)
                sums[:, at] += terms[u]
            return carry

        lax.fori_loop(1, lax.div(need + 1, 2), more, 0)


def halo_kernel(acc, old0, old1, r0, r1, tiles, tab, s0, s1, halo, sums, *, cheb, slots):
    edge = GHOST * TB
    halo_products(acc, r0, r1, tiles, tab, halo, sums, slots)
    for side, old, new in ((0, old0, s0), (1, old1, s1)):
        value = sums[:, side * edge : (side + 1) * edge]
        if cheb:
            value = 2.0 * value - old[...].astype(jnp.float32)
        new[...] = value.astype(jnp.bfloat16)


def halo_last_kernel(acc, s0, s1, r0, r1, tiles, tab, both, keep, give, whole, halo, sums, *, slots):
    edge = GHOST * TB
    size = both.shape[0]
    halo_products(acc, r0, r1, tiles, tab, halo, sums, slots)
    cross = both[:, size:]
    for side, y in ((0, s0), (1, s1)):
        image = sums[:, side * edge : (side + 1) * edge].astype(jnp.bfloat16)
        cross = cross + lax.dot_general(y[...], image, NT_DIMS, preferred_element_type=jnp.float32)
    whole[...] = jnp.concatenate([both[:, :size], cross], axis=1)
    half = size // 2
    mine = pl.multiple_of(tab[MISC, 2] * half, half)
    keep[...] = whole[pl.ds(mine, half), :]
    give[...] = whole[pl.ds(pl.multiple_of(half - mine, half), half), :]


def eliminate(gram):
    size = gram.shape[0]
    step, sub = 8, 8
    lanes = lax.broadcasted_iota(jnp.int32, (sub, 2 * size), 1)
    inner = lax.broadcasted_iota(jnp.int32, (sub, 2 * size), 0)
    wide = jnp.concatenate([gram, jnp.zeros_like(gram)], axis=1)
    work = [
        jnp.where(lanes == inner + g * sub + size, 1.0, wide[g * sub : (g + 1) * sub]) for g in range(size // sub)
    ]
    for k in range(0, size, step):
        g0, off = divmod(k, sub)
        cols = [
            {g: jnp.broadcast_to(work[g][:, k + j : k + j + 1], (sub, 2 * size)) for g in range(g0, size // sub)}
            for j in range(step)
        ]
        rows = [work[g0][off + j : off + j + 1] for j in range(step)]
        units = []
        finals = []
        for j in range(step):
            pivot = cols[j][g0][off + j : off + j + 1]
            inverse = 1.0 / pivot
            unit = rows[j] * inverse
            units.append(unit)
            finals.append(rows[j] * lax.rsqrt(pivot))
            for m in range(j + 1, step):
                rows[m] = rows[m] - cols[j][g0][off + m : off + m + 1] * unit
                factor = cols[m][g0][off + j : off + j + 1] * inverse
                cols[m] = {g: cols[m][g] - cols[j][g] * factor for g in cols[m]}
        for g in range(g0, size // sub):
            value = work[g]
            for j in range(step):
                value = value - cols[j][g] * units[j]
            if g == g0:
                value = jnp.where(inner >= off + step, value, work[g])
                for j in range(step):
                    value = jnp.where(inner == off + j, finals[j], value)
            work[g] = value
    return jnp.concatenate(work, axis=0)[:, size:]


def split3(x):
    hi = x.astype(jnp.bfloat16)
    rest = x - hi.astype(jnp.float32)
    mid = rest.astype(jnp.bfloat16)
    low = (rest - mid.astype(jnp.float32)).astype(jnp.bfloat16)
    return hi, mid, low


def end_kernel(mine, other, s0, mid, s1, tab, basis, projected, both, *, nodes_all):
    size = both.shape[0]
    half = size // 2
    at = pl.multiple_of(tab[MISC, 2] * half, half)
    both[pl.ds(at, half), :] = mine[...]
    both[pl.ds(pl.multiple_of(half - at, half), half), :] = other[...]
    edge, inner = s0.shape[1], mid.shape[1]
    values = both[...] / nodes_all
    inverse = eliminate(values[:, :size])
    cross = values[:, size:]
    parts = jnp.concatenate(split3(inverse), axis=0)

    def piece(y):
        out = jnp.dot(parts, y, preferred_element_type=jnp.float32)
        return (out[:size] + (out[size : 2 * size] + out[2 * size :])).astype(jnp.bfloat16)

    lead = pl.multiple_of(tab[MISC, 0] * TB, TB)
    trail = pl.multiple_of(tab[MISC, 1] * TB, TB)
    basis[:, pl.ds(lead, edge)] = piece(s0[...])
    basis[:, pl.ds(trail, edge)] = piece(s1[...])
    for c in range(0, inner, edge):
        basis[:, edge + c : 2 * edge + c] = piece(mid[:, c : c + edge])
    half = jnp.dot(inverse, cross, precision=lax.Precision.HIGHEST, preferred_element_type=jnp.float32)
    projected[...] = lax.dot_general(
        half, inverse, NT_DIMS, precision=lax.Precision.HIGHEST, preferred_element_type=jnp.float32
    )


def rotations(shape, axis):
    at = np.arange(int(np.prod(shape))).reshape(shape)
    return [
        list(zip(at.reshape(-1).tolist(), np.roll(at, -k, axis=axis).reshape(-1).tolist()))
        for k in range(1, shape[axis])
    ]


def all_sum(keep, give, dom, board):
    shape = (dom // 8, 4, 2, board)
    (swap,) = rotations(shape, 2)
    x = keep + lax.ppermute(give, AX, swap)
    planes = np.arange(dom * board).reshape(-1, 2 * board).T.tolist()
    spread = jnp.broadcast_to(x[None], (dom // 2,) + x.shape)
    x = lax.all_to_all(spread, AX, 0, 0, axis_index_groups=planes).sum(0)
    spread = jnp.broadcast_to(x[None], (board,) + x.shape)
    x = lax.all_to_all(spread, "board", 0, 0).sum(0)
    return x, lax.ppermute(x, AX, swap)


def body(block, tiles, cols, counts, *, dom, board):
    devices = dom * board
    size, wide = block.shape
    rows, slots = cols.shape
    edge = GHOST * TB
    inner = wide - 2 * edge
    bf16, f32 = jnp.bfloat16, jnp.float32
    shape = jax.ShapeDtypeStruct
    me = lax.axis_index(AX)
    odd = me % 2

    even_pairs = [(i, i ^ 1) for i in range(devices)]
    odd_pairs = [(i, (((i + 1) ^ 1) - 1) % devices) for i in range(devices)]
    last_pairs = [(0, 0)] + odd_pairs[1:-1] + [(devices - 1, devices - 1)]

    def exchange(s0, s1, odd_pairs=odd_pairs):
        return lax.ppermute(s0, AX, even_pairs), lax.ppermute(s1, AX, odd_pairs)

    head, tail = block[:, :edge], block[:, wide - edge :]
    s0, s1 = jnp.where(odd == 1, head, tail), jnp.where(odd == 1, tail, head)
    r0, r1 = exchange(s0, s1)

    own_flops = 2 * rows * slots * size * TB * TB
    halo_flops = own_flops // 8
    acc_shape = shape((size, 2 * edge), f32)
    mid_shape = shape((size, inner), bf16)
    edge_shape = shape((size, edge), bf16)
    field = pltpu.VMEM((size, wide + TB), bf16)
    halo_scratch = [pltpu.VMEM((size, 2 * edge + TB), bf16), pltpu.VMEM((size, 2 * edge), f32)]

    tiles_v, acc, mid, new, tab = call(
        functools.partial(load_kernel, board=board),
        [shape((rows, slots * TB, TB), bf16), acc_shape, mid_shape, mid_shape, pltpu.SMEM(TABLE, jnp.int32)],
        [VM, VM, HBM, HBM, HBM, HBM],
        [VM, VM, VM, VM, SM],
        [
            field,
            pltpu.VMEM(tiles.shape, bf16),
            pltpu.VMEM((slots, rows), jnp.int32),
            pltpu.VMEM((1, rows), jnp.int32),
            pltpu.VMEM(TABLE, jnp.int32),
            pltpu.SemaphoreType.DMA((rows // GROUP,)),
            pltpu.SemaphoreType.DMA((4,)),
        ],
        limit=40,
        flops=own_flops,
        bytes_=tiles.size * 2,
    )(s0, s1, *(stay(v) for v in (block, tiles, cols.T, counts.reshape(1, rows))))

    tab = pltpu.with_memory_space_constraint(tab, pltpu.SMEM)
    older = (s0, mid, s1)
    for degree in range(DEG):
        old0, old_mid, old1 = older
        older = (s0, mid, s1)
        s0, s1 = call(
            functools.partial(halo_kernel, cheb=degree > 0, slots=slots),
            [edge_shape, edge_shape],
            [VM, VM, VM, VM, VM, VM, SM],
            [VM, VM],
            halo_scratch,
            flops=halo_flops,
        )(acc, old0, old1, r0, r1, tiles_v, tab)
        mid = new
        r0, r1 = exchange(s0, s1, odd_pairs if degree < DEG - 1 else last_pairs)
        if degree < DEG - 1:
            acc, new = call(
                functools.partial(own_kernel, slots=slots),
                [acc_shape, mid_shape],
                [VM, VM, VM, VM, VM, SM],
                [VM, VM],
                [field],
                flops=own_flops,
            )(s0, mid, s1, older[1], tiles_v, tab)
        else:
            acc, both = call(
                functools.partial(own_last_kernel, slots=slots),
                [acc_shape, shape((size, 2 * size), f32)],
                [VM, VM, VM, VM, SM],
                [VM, VM],
                [field, pltpu.VMEM((size, inner), bf16)],
                flops=own_flops,
            )(s0, mid, s1, tiles_v, tab)

    half_shape = shape((size // 2, 2 * size), f32)
    keep, give = call(
        functools.partial(halo_last_kernel, slots=slots),
        [half_shape, half_shape],
        [VM, VM, VM, VM, VM, VM, SM, VM],
        [VM, VM],
        [pltpu.VMEM((size, 2 * size), f32)] + halo_scratch,
        flops=halo_flops,
    )(acc, s0, s1, r0, r1, tiles_v, tab, both)
    mine, other = all_sum(keep, give, dom, board)
    basis, projected = call(
        functools.partial(end_kernel, nodes_all=devices * rows * TB),
        [shape((size, wide), bf16), shape((size, size), f32)],
        [VM, VM, VM, VM, VM, SM],
        [VM, VM],
        [pltpu.VMEM((size, 2 * size), f32)],
        flops=6 * size * size * wide,
    )(mine, other, s0, mid, s1, tab)
    return basis, projected


def solution(mesh):
    dom, board = mesh.shape["dom"], mesh.shape["board"]
    return jax.shard_map(
        functools.partial(body, dom=dom, board=board),
        mesh=mesh,
        in_specs=(
            P(None, AX),
            P(AX, None, None, None),
            P(AX, None),
            P(AX),
        ),
        out_specs=(P(None, AX), P()),
        check_vma=False,
    )
```

```python
import functools

import jax
import jax.numpy as jnp
import numpy as np
from jax import lax
from jax.experimental import pallas as pl
from jax.experimental.pallas import tpu as pltpu
from jax.sharding import PartitionSpec as P

DEG = 4
GHOST = 8
TB = 128
AX = ("dom", "board")
MIB = 1 << 20
NN_DIMS = (((1,), (0,)), ((), ()))
NT_DIMS = (((1,), (1,)), ((), ()))
GROUP = 8
SMALL = 4

VM = pl.BlockSpec(memory_space=pltpu.VMEM)
SM = pl.BlockSpec(memory_space=pltpu.SMEM)
HBM = pl.BlockSpec(memory_space=pltpu.HBM)

OWN, SLOT, BLOCK, NEED, MISC = 0, 10, 20, 30, 31
TABLE = (32, 128)


def call(kernel, out_shape, in_specs, out_specs, scratch=(), limit=24, flops=0, bytes_=0):
    return pl.pallas_call(
        kernel,
        out_shape=out_shape,
        in_specs=in_specs,
        out_specs=out_specs,
        scratch_shapes=scratch,
        compiler_params=pltpu.CompilerParams(vmem_limit_bytes=limit * MIB),
        cost_estimate=pl.CostEstimate(flops=flops, bytes_accessed=bytes_, transcendentals=0),
    )


def stay(x):
    return pltpu.with_memory_space_constraint(x, pltpu.HBM)


def block_at(ref, offset):
    return ref[:, pl.ds(pl.multiple_of(offset, TB), TB)]


def own_row(src, tiles, tab, row, slots):
    total = None
    for pair in range(slots // 2):
        lhs = jnp.concatenate(
            [block_at(src, tab[OWN + 2 * pair, row]), block_at(src, tab[OWN + 2 * pair + 1, row])], axis=1
        )
        rhs = tiles(row, pair)
        term = lax.dot_general(lhs, rhs, NN_DIMS, preferred_element_type=jnp.float32)
        total = term if total is None else total + term
    return total


def gather_field(src, s0, mid, s1):
    edge, inner = s0.shape[1], mid.shape[1]
    src[:, :edge] = s0[...]
    src[:, edge : edge + inner] = mid[...]
    src[:, edge + inner : 2 * edge + inner] = s1[...]
    src[:, 2 * edge + inner :] = jnp.zeros_like(src[:, 2 * edge + inner :])


def own_products(src, pair_of, tab, old, acc, new, cheb, slots, rows, before=None, group=GROUP):
    def place(u, value):
        at = pl.ds(pl.multiple_of(u * TB, TB), TB)
        if cheb:
            value = 2.0 * value - old[:, at].astype(jnp.float32)
        new[:, at] = value.astype(jnp.bfloat16)

    def side(u, value):
        acc[:, pl.ds(pl.multiple_of(u * TB, TB), TB)] = value

    def sweep(first, out, count, store):
        def step(g, carry):
            if before is not None:
                before(first + g * group)
            values = [own_row(src, pair_of, tab, first + g * group + u, slots) for u in range(group)]
            for u in range(group):
                store(out + g * group + u, values[u])
            return carry

        lax.fori_loop(0, count // group, step, 0)

    lead, trail = tab[MISC, 0], tab[MISC, 1]
    sweep(lead, 0, GHOST, side)
    sweep(GHOST, 0, rows - 2 * GHOST, place)
    sweep(trail, GHOST, GHOST, side)


def held_pairs(tiles):
    return lambda row, pair: tiles[row, 2 * pair * TB : 2 * (pair + 1) * TB, :]


def fill_table(cols, counts, place, lines, rows, slots):
    first, odd, core = place[0], place[1], place[2]
    lead = (1 - odd) * (rows - GHOST)
    near = cols[...] - first
    live = lax.broadcasted_iota(jnp.int32, near.shape, 0) < counts[...]
    inside = (near >= 0) & (near < rows)
    spot = jnp.where(near < GHOST, near + lead, jnp.where(near >= rows - GHOST, near - lead, near))
    lines[OWN : OWN + slots, :rows] = jnp.where(live & inside, spot, rows) * TB
    out = jnp.where(live & ~inside, 1, 0)
    there = jnp.where(near < 0, near + GHOST + GHOST * (1 - odd), near - rows + GHOST * odd) * TB
    empty = jnp.zeros((1, rows), jnp.int32)
    found = empty
    slot_lines, block_lines = [empty] * slots, [empty + 2 * GHOST * TB] * slots
    for s in range(slots):
        here = out[s : s + 1]
        for q in range(s + 1):
            hit = (here == 1) & (found == q)
            slot_lines[q] = jnp.where(hit, s * TB, slot_lines[q])
            block_lines[q] = jnp.where(hit, there[s : s + 1], block_lines[q])
        found = found + here
    for q in range(slots):
        lines[SLOT + q : SLOT + q + 1, :rows] = slot_lines[q]
        lines[BLOCK + q : BLOCK + q + 1, :rows] = block_lines[q]
    lines[NEED : NEED + 1, :rows] = found
    lane = lax.broadcasted_iota(jnp.int32, (1, rows), 1)
    lines[MISC : MISC + 1, :rows] = jnp.where(lane == 0, lead, jnp.where(lane == 1, rows - GHOST - lead, core))


def load_kernel(
    s0, s1, block, tiles_hbm, cols_hbm, counts_hbm, tiles, acc, mid0, new, tab, src, raw, cols, counts, lines,
    sems, small_sems, *, board,
):
    rows, slots = raw.shape[0], raw.shape[1]
    edge = GHOST * TB
    chunk = GROUP
    me = lax.axis_index(AX)
    place = (me * rows, lax.rem(me, 2), lax.rem(lax.div(me, board), 2))
    little = [
        pltpu.make_async_copy(cols_hbm, cols, small_sems.at[0]),
        pltpu.make_async_copy(counts_hbm, counts, small_sems.at[1]),
        pltpu.make_async_copy(block.at[:, pl.ds(edge, mid0.shape[1])], mid0, small_sems.at[2]),
    ]
    for copy in little:
        copy.start()

    def piece(start):
        return pltpu.make_async_copy(
            tiles_hbm.at[pl.ds(start, chunk)], raw.at[pl.ds(start, chunk)], sems.at[lax.div(start, chunk)]
        )

    lead = (1 - place[1]) * (rows - GHOST)
    for c in range(GHOST // chunk):
        piece(lead + c * chunk).start()
    for c in range(GHOST // chunk, (rows - GHOST) // chunk):
        piece(c * chunk).start()
    for c in range(GHOST // chunk):
        piece(rows - GHOST - lead + c * chunk).start()
    little[0].wait()
    little[1].wait()
    fill_table(cols, counts, place, lines, rows, slots)
    to_scalars = pltpu.make_async_copy(lines, tab, small_sems.at[3])
    to_scalars.start()
    little[2].wait()
    gather_field(src, s0, mid0, s1)
    to_scalars.wait()

    def pair_of(row, pair):
        turned = jnp.concatenate([raw[row, 2 * pair].T, raw[row, 2 * pair + 1].T], axis=0)
        tiles[row, 2 * pair * TB : 2 * (pair + 1) * TB, :] = turned
        return turned

    own_products(
        src, pair_of, tab, None, acc, new, False, slots, rows, before=lambda start: piece(start).wait(), group=chunk
    )


def own_kernel(s1, mid, s0, old, tiles, tab, acc, new, src, *, slots):
    gather_field(src, s0, mid, s1)
    own_products(src, held_pairs(tiles), tab, old, acc, new, True, slots, tiles.shape[0])


def own_last_kernel(s1, mid, s0, tiles, tab, acc, both, src, new, *, slots):
    gather_field(src, s0, mid, s1)
    own_products(src, held_pairs(tiles), tab, None, acc, new, False, slots, tiles.shape[0])
    edge, inner = s0.shape[1], mid.shape[1]
    size = mid.shape[0]
    mids = mid[...]
    total = lax.dot_general(
        mids, jnp.concatenate([mids, new[...]], axis=0), NT_DIMS, preferred_element_type=jnp.float32
    )
    gram = jnp.zeros((size, size), jnp.float32)
    for side in (s0[...], s1[...]):
        gram = gram + lax.dot_general(side, side, NT_DIMS, preferred_element_type=jnp.float32)
    both[...] = total + jnp.concatenate([gram, jnp.zeros_like(gram)], axis=1)


def halo_products(acc, r0, r1, tiles, tab, halo, sums, slots):
    edge = GHOST * TB
    halo[:, :edge] = r0[...]
    halo[:, edge : 2 * edge] = r1[...]
    halo[:, 2 * edge :] = jnp.zeros_like(halo[:, 2 * edge :])

    first = (tab[MISC, 0], tab[MISC, 1])

    def term(k, pair):
        row = first[k // GHOST] + k % GHOST
        lhs = jnp.concatenate(
            [block_at(halo, tab[BLOCK + 2 * pair, row]), block_at(halo, tab[BLOCK + 2 * pair + 1, row])], axis=1
        )
        rhs = jnp.concatenate(
            [tiles[row, pl.ds(pl.multiple_of(tab[SLOT + 2 * pair + e, row], TB), TB), :] for e in (0, 1)], axis=0
        )
        return lax.dot_general(lhs, rhs, NN_DIMS, preferred_element_type=jnp.float32)

    for half in (0, GHOST):
        terms = [term(half + u, 0) for u in range(GHOST)]
        for u in range(GHOST):
            at = slice((half + u) * TB, (half + u + 1) * TB)
            sums[:, at] = acc[:, at] + terms[u]
    for g in range(2 * GHOST // SMALL):
        start = first[g * SMALL // GHOST] + g * SMALL % GHOST
        need = tab[NEED, start]
        for u in range(1, SMALL):
            need = jnp.maximum(need, tab[NEED, start + u])

        def more(pair, carry, g=g):
            terms = [term(g * SMALL + u, pair) for u in range(SMALL)]
            for u in range(SMALL):
                at = slice((g * SMALL + u) * TB, (g * SMALL + u + 1) * TB)
                sums[:, at] += terms[u]
            return carry

        lax.fori_loop(1, lax.div(need + 1, 2), more, 0)


def halo_kernel(acc, old0, old1, r0, r1, tiles, tab, s1, s0, halo, sums, *, cheb, slots):
    edge = GHOST * TB
    halo_products(acc, r0, r1, tiles, tab, halo, sums, slots)
    for side, old, new in ((0, old0, s0), (1, old1, s1)):
        value = sums[:, side * edge : (side + 1) * edge]
        if cheb:
            value = 2.0 * value - old[...].astype(jnp.float32)
        new[...] = value.astype(jnp.bfloat16)


def halo_last_kernel(acc, s0, s1, r0, r1, tiles, tab, both, keep, give, whole, halo, sums, *, slots):
    edge = GHOST * TB
    size = both.shape[0]
    halo_products(acc, r0, r1, tiles, tab, halo, sums, slots)
    cross = both[:, size:]
    for side, y in ((0, s0), (1, s1)):
        image = sums[:, side * edge : (side + 1) * edge].astype(jnp.bfloat16)
        cross = cross + lax.dot_general(y[...], image, NT_DIMS, preferred_element_type=jnp.float32)
    whole[...] = jnp.concatenate([both[:, :size], cross], axis=1)
    half = size // 2
    mine = pl.multiple_of(tab[MISC, 2] * half, half)
    keep[...] = whole[pl.ds(mine, half), :]
    give[...] = whole[pl.ds(pl.multiple_of(half - mine, half), half), :]


def eliminate(gram):
    size = gram.shape[0]
    step, sub = 8, 8
    lanes = lax.broadcasted_iota(jnp.int32, (sub, 2 * size), 1)
    inner = lax.broadcasted_iota(jnp.int32, (sub, 2 * size), 0)
    wide = jnp.concatenate([gram, jnp.zeros_like(gram)], axis=1)
    work = [
        jnp.where(lanes == inner + g * sub + size, 1.0, wide[g * sub : (g + 1) * sub]) for g in range(size // sub)
    ]
    for k in range(0, size, step):
        g0, off = divmod(k, sub)
        cols = [
            {g: jnp.broadcast_to(work[g][:, k + j : k + j + 1], (sub, 2 * size)) for g in range(g0, size // sub)}
            for j in range(step)
        ]
        rows = [work[g0][off + j : off + j + 1] for j in range(step)]
        units = []
        finals = []
        for j in range(step):
            pivot = cols[j][g0][off + j : off + j + 1]
            inverse = 1.0 / pivot
            unit = rows[j] * inverse
            units.append(unit)
            finals.append(rows[j] * lax.rsqrt(pivot))
            for m in range(j + 1, step):
                rows[m] = rows[m] - cols[j][g0][off + m : off + m + 1] * unit
                factor = cols[m][g0][off + j : off + j + 1] * inverse
                cols[m] = {g: cols[m][g] - cols[j][g] * factor for g in cols[m]}
        for g in range(g0, size // sub):
            value = work[g]
            for j in range(step):
                value = value - cols[j][g] * units[j]
            if g == g0:
                value = jnp.where(inner >= off + step, value, work[g])
                for j in range(step):
                    value = jnp.where(inner == off + j, finals[j], value)
            work[g] = value
    return jnp.concatenate(work, axis=0)[:, size:]


def split3(x):
    hi = x.astype(jnp.bfloat16)
    rest = x - hi.astype(jnp.float32)
    mid = rest.astype(jnp.bfloat16)
    low = (rest - mid.astype(jnp.float32)).astype(jnp.bfloat16)
    return hi, mid, low


def end_kernel(mine, other, s0, mid, s1, tab, basis, projected, both, *, nodes_all):
    size = both.shape[0]
    half = size // 2
    at = pl.multiple_of(tab[MISC, 2] * half, half)
    both[pl.ds(at, half), :] = mine[...]
    both[pl.ds(pl.multiple_of(half - at, half), half), :] = other[...]
    edge, inner = s0.shape[1], mid.shape[1]
    values = both[...] / nodes_all
    inverse = eliminate(values[:, :size])
    cross = values[:, size:]
    parts = jnp.concatenate(split3(inverse), axis=0)

    def piece(y):
        out = jnp.dot(parts, y, preferred_element_type=jnp.float32)
        return (out[:size] + (out[size : 2 * size] + out[2 * size :])).astype(jnp.bfloat16)

    lead = pl.multiple_of(tab[MISC, 0] * TB, TB)
    trail = pl.multiple_of(tab[MISC, 1] * TB, TB)
    basis[:, pl.ds(lead, edge)] = piece(s0[...])
    basis[:, pl.ds(trail, edge)] = piece(s1[...])
    for c in range(0, inner, edge):
        basis[:, edge + c : 2 * edge + c] = piece(mid[:, c : c + edge])
    half = jnp.dot(inverse, cross, precision=lax.Precision.HIGHEST, preferred_element_type=jnp.float32)
    projected[...] = lax.dot_general(
        half, inverse, NT_DIMS, precision=lax.Precision.HIGHEST, preferred_element_type=jnp.float32
    )


def rotations(shape, axis):
    at = np.arange(int(np.prod(shape))).reshape(shape)
    return [
        list(zip(at.reshape(-1).tolist(), np.roll(at, -k, axis=axis).reshape(-1).tolist()))
        for k in range(1, shape[axis])
    ]


def all_sum(keep, give, dom, board):
    shape = (dom // 8, 4, 2, board)
    (swap,) = rotations(shape, 2)
    x = keep + lax.ppermute(give, AX, swap)
    planes = np.arange(dom * board).reshape(-1, 2 * board).T.tolist()
    spread = jnp.broadcast_to(x[None], (dom // 2,) + x.shape)
    x = lax.all_to_all(spread, AX, 0, 0, axis_index_groups=planes).sum(0)
    spread = jnp.broadcast_to(x[None], (board,) + x.shape)
    x = lax.all_to_all(spread, "board", 0, 0).sum(0)
    return x, lax.ppermute(x, AX, swap)


def body(block, tiles, cols, counts, *, dom, board):
    devices = dom * board
    size, wide = block.shape
    rows, slots = cols.shape
    edge = GHOST * TB
    inner = wide - 2 * edge
    bf16, f32 = jnp.bfloat16, jnp.float32
    shape = jax.ShapeDtypeStruct
    me = lax.axis_index(AX)
    odd = me % 2

    even_pairs = [(i, i ^ 1) for i in range(devices)]
    odd_pairs = [(i, (((i + 1) ^ 1) - 1) % devices) for i in range(devices)]
    last_pairs = [(0, 0)] + odd_pairs[1:-1] + [(devices - 1, devices - 1)]

    def exchange(s0, s1, odd_pairs=odd_pairs):
        r1 = lax.ppermute(s1, AX, odd_pairs)
        r0 = lax.ppermute(s0, AX, even_pairs)
        return r0, r1

    head, tail = block[:, :edge], block[:, wide - edge :]
    s0, s1 = jnp.where(odd == 1, head, tail), jnp.where(odd == 1, tail, head)
    r0, r1 = exchange(s0, s1)

    own_flops = 2 * rows * slots * size * TB * TB
    halo_flops = own_flops // 8
    acc_shape = shape((size, 2 * edge), f32)
    mid_shape = shape((size, inner), bf16)
    edge_shape = shape((size, edge), bf16)
    field = pltpu.VMEM((size, wide + TB), bf16)
    halo_scratch = [pltpu.VMEM((size, 2 * edge + TB), bf16), pltpu.VMEM((size, 2 * edge), f32)]

    tiles_v, acc, mid, new, tab = call(
        functools.partial(load_kernel, board=board),
        [shape((rows, slots * TB, TB), bf16), acc_shape, mid_shape, mid_shape, pltpu.SMEM(TABLE, jnp.int32)],
        [VM, VM, HBM, HBM, HBM, HBM],
        [VM, VM, VM, VM, SM],
        [
            field,
            pltpu.VMEM(tiles.shape, bf16),
            pltpu.VMEM((slots, rows), jnp.int32),
            pltpu.VMEM((1, rows), jnp.int32),
            pltpu.VMEM(TABLE, jnp.int32),
            pltpu.SemaphoreType.DMA((rows // GROUP,)),
            pltpu.SemaphoreType.DMA((4,)),
        ],
        limit=40,
        flops=own_flops,
        bytes_=tiles.size * 2,
    )(s0, s1, *(stay(v) for v in (block, tiles, cols.T, counts.reshape(1, rows))))

    tab = pltpu.with_memory_space_constraint(tab, pltpu.SMEM)
    older = (s0, mid, s1)
    for degree in range(DEG):
        old0, old_mid, old1 = older
        older = (s0, mid, s1)
        s1, s0 = call(
            functools.partial(halo_kernel, cheb=degree > 0, slots=slots),
            [edge_shape, edge_shape],
            [VM, VM, VM, VM, VM, VM, SM],
            [VM, VM],
            halo_scratch,
            flops=halo_flops,
        )(acc, old0, old1, r0, r1, tiles_v, tab)
        mid = new
        r0, r1 = exchange(s0, s1, odd_pairs if degree < DEG - 1 else last_pairs)
        if degree < DEG - 1:
            acc, new = call(
                functools.partial(own_kernel, slots=slots),
                [acc_shape, mid_shape],
                [VM, VM, VM, VM, VM, SM],
                [VM, VM],
                [field],
                flops=own_flops,
            )(s1, mid, s0, older[1], tiles_v, tab)
        else:
            acc, both = call(
                functools.partial(own_last_kernel, slots=slots),
                [acc_shape, shape((size, 2 * size), f32)],
                [VM, VM, VM, VM, SM],
                [VM, VM],
                [field, pltpu.VMEM((size, inner), bf16)],
                flops=own_flops,
            )(s1, mid, s0, tiles_v, tab)

    half_shape = shape((size // 2, 2 * size), f32)
    keep, give = call(
        functools.partial(halo_last_kernel, slots=slots),
        [half_shape, half_shape],
        [VM, VM, VM, VM, VM, VM, SM, VM],
        [VM, VM],
        [pltpu.VMEM((size, 2 * size), f32)] + halo_scratch,
        flops=halo_flops,
    )(acc, s0, s1, r0, r1, tiles_v, tab, both)
    mine, other = all_sum(keep, give, dom, board)
    basis, projected = call(
        functools.partial(end_kernel, nodes_all=devices * rows * TB),
        [shape((size, wide), bf16), shape((size, size), f32)],
        [VM, VM, VM, VM, VM, SM],
        [VM, VM],
        [pltpu.VMEM((size, 2 * size), f32)],
        flops=6 * size * size * wide,
    )(mine, other, s0, mid, s1, tab)
    return basis, projected


def solution(mesh):
    dom, board = mesh.shape["dom"], mesh.shape["board"]
    return jax.shard_map(
        functools.partial(body, dom=dom, board=board),
        mesh=mesh,
        in_specs=(
            P(None, AX),
            P(AX, None, None, None),
            P(AX, None),
            P(AX),
        ),
        out_specs=(P(None, AX), P()),
        check_vma=False,
    )
```

```python
import functools

import jax
import jax.numpy as jnp
import numpy as np
from jax import lax
from jax.experimental import pallas as pl
from jax.experimental.pallas import tpu as pltpu
from jax.sharding import PartitionSpec as P

DEG = 4
GHOST = 8
TB = 128
AX = ("dom", "board")
MIB = 1 << 20
NN_DIMS = (((1,), (0,)), ((), ()))
NT_DIMS = (((1,), (1,)), ((), ()))
GROUP = 8
SMALL = 4

VM = pl.BlockSpec(memory_space=pltpu.VMEM)
SM = pl.BlockSpec(memory_space=pltpu.SMEM)
HBM = pl.BlockSpec(memory_space=pltpu.HBM)

OWN, SLOT, BLOCK, NEED, MISC = 0, 10, 20, 30, 31
TABLE = (32, 128)


def call(kernel, out_shape, in_specs, out_specs, scratch=(), limit=24, flops=0, bytes_=0):
    return pl.pallas_call(
        kernel,
        out_shape=out_shape,
        in_specs=in_specs,
        out_specs=out_specs,
        scratch_shapes=scratch,
        compiler_params=pltpu.CompilerParams(vmem_limit_bytes=limit * MIB),
        cost_estimate=pl.CostEstimate(flops=flops, bytes_accessed=bytes_, transcendentals=0),
    )


def stay(x):
    return pltpu.with_memory_space_constraint(x, pltpu.HBM)


def block_at(ref, offset):
    return ref[:, pl.ds(pl.multiple_of(offset, TB), TB)]


def own_row(src, tiles, tab, row, slots):
    total = None
    for pair in range(slots // 2):
        lhs = jnp.concatenate(
            [block_at(src, tab[OWN + 2 * pair, row]), block_at(src, tab[OWN + 2 * pair + 1, row])], axis=1
        )
        rhs = tiles(row, pair)
        term = lax.dot_general(lhs, rhs, NN_DIMS, preferred_element_type=jnp.float32)
        total = term if total is None else total + term
    return total


def gather_field(src, s0, mid, s1):
    edge, inner = s0.shape[1], mid.shape[1]
    src[:, :edge] = s0[...]
    src[:, edge : edge + inner] = mid[...]
    src[:, edge + inner : 2 * edge + inner] = s1[...]
    src[:, 2 * edge + inner :] = jnp.zeros_like(src[:, 2 * edge + inner :])


def own_products(src, pair_of, tab, old, acc, new, cheb, slots, rows, before=None, group=GROUP):
    def place(u, value):
        at = pl.ds(pl.multiple_of(u * TB, TB), TB)
        if cheb:
            value = 2.0 * value - old[:, at].astype(jnp.float32)
        new[:, at] = value.astype(jnp.bfloat16)

    def side(u, value):
        acc[:, pl.ds(pl.multiple_of(u * TB, TB), TB)] = value

    def sweep(first, out, count, store):
        def step(g, carry):
            if before is not None:
                before(first + g * group)
            values = [own_row(src, pair_of, tab, first + g * group + u, slots) for u in range(group)]
            for u in range(group):
                store(out + g * group + u, values[u])
            return carry

        lax.fori_loop(0, count // group, step, 0)

    lead, trail = tab[MISC, 0], tab[MISC, 1]
    sweep(lead, 0, GHOST, side)
    sweep(GHOST, 0, rows - 2 * GHOST, place)
    sweep(trail, GHOST, GHOST, side)


def held_pairs(tiles):
    return lambda row, pair: tiles[row, 2 * pair * TB : 2 * (pair + 1) * TB, :]


def fill_table(cols, counts, place, lines, rows, slots):
    first, odd, core = place[0], place[1], place[2]
    lead = (1 - odd) * (rows - GHOST)
    near = cols[...] - first
    live = lax.broadcasted_iota(jnp.int32, near.shape, 0) < counts[...]
    inside = (near >= 0) & (near < rows)
    spot = jnp.where(near < GHOST, near + lead, jnp.where(near >= rows - GHOST, near - lead, near))
    lines[OWN : OWN + slots, :rows] = jnp.where(live & inside, spot, rows) * TB
    out = jnp.where(live & ~inside, 1, 0)
    there = jnp.where(near < 0, near + GHOST + GHOST * (1 - odd), near - rows + GHOST * odd) * TB
    empty = jnp.zeros((1, rows), jnp.int32)
    found = empty
    slot_lines, block_lines = [empty] * slots, [empty + 2 * GHOST * TB] * slots
    for s in range(slots):
        here = out[s : s + 1]
        for q in range(s + 1):
            hit = (here == 1) & (found == q)
            slot_lines[q] = jnp.where(hit, s * TB, slot_lines[q])
            block_lines[q] = jnp.where(hit, there[s : s + 1], block_lines[q])
        found = found + here
    for q in range(slots):
        lines[SLOT + q : SLOT + q + 1, :rows] = slot_lines[q]
        lines[BLOCK + q : BLOCK + q + 1, :rows] = block_lines[q]
    lines[NEED : NEED + 1, :rows] = found
    lane = lax.broadcasted_iota(jnp.int32, (1, rows), 1)
    lines[MISC : MISC + 1, :rows] = jnp.where(lane == 0, lead, jnp.where(lane == 1, rows - GHOST - lead, jnp.where(lane == 2, core, place[3])))


def load_kernel(
    s0, s1, block, tiles_hbm, cols_hbm, counts_hbm, tiles, acc, mid0, new, tab, src, raw, cols, counts, lines,
    sems, small_sems, *, board,
):
    rows, slots = raw.shape[0], raw.shape[1]
    edge = GHOST * TB
    chunk = GROUP
    me = lax.axis_index(AX)
    turn = 8 * board
    apart = jnp.where((me == turn - 1) | (me == turn), 1, 0)
    place = (me * rows, lax.rem(me, 2), lax.rem(lax.div(me, board), 2), apart)
    little = [
        pltpu.make_async_copy(cols_hbm, cols, small_sems.at[0]),
        pltpu.make_async_copy(counts_hbm, counts, small_sems.at[1]),
        pltpu.make_async_copy(block.at[:, pl.ds(edge, mid0.shape[1])], mid0, small_sems.at[2]),
    ]
    for copy in little:
        copy.start()

    def piece(start):
        return pltpu.make_async_copy(
            tiles_hbm.at[pl.ds(start, chunk)], raw.at[pl.ds(start, chunk)], sems.at[lax.div(start, chunk)]
        )

    lead = (1 - place[1]) * (rows - GHOST)
    for c in range(GHOST // chunk):
        piece(lead + c * chunk).start()
    for c in range(GHOST // chunk, (rows - GHOST) // chunk):
        piece(c * chunk).start()
    for c in range(GHOST // chunk):
        piece(rows - GHOST - lead + c * chunk).start()
    little[0].wait()
    little[1].wait()
    fill_table(cols, counts, place, lines, rows, slots)
    to_scalars = pltpu.make_async_copy(lines, tab, small_sems.at[3])
    to_scalars.start()
    little[2].wait()
    gather_field(src, s0, mid0, s1)
    to_scalars.wait()

    def pair_of(row, pair):
        turned = jnp.concatenate([raw[row, 2 * pair].T, raw[row, 2 * pair + 1].T], axis=0)
        tiles[row, 2 * pair * TB : 2 * (pair + 1) * TB, :] = turned
        return turned

    own_products(
        src, pair_of, tab, None, acc, new, False, slots, rows, before=lambda start: piece(start).wait(), group=chunk
    )


def own_kernel(s1, mid, s0, old, tiles, tab, acc, new, src, *, slots):
    gather_field(src, s0, mid, s1)
    own_products(src, held_pairs(tiles), tab, old, acc, new, True, slots, tiles.shape[0])


def own_last_kernel(s2, s1, mid, s0, tiles, tab, acc, both, src, new, *, slots):
    gather_field(src, s0, mid, s1)
    own_products(src, held_pairs(tiles), tab, None, acc, new, False, slots, tiles.shape[0])
    edge, inner = s0.shape[1], mid.shape[1]
    size = mid.shape[0]
    mids = mid[...]
    total = lax.dot_general(
        mids, jnp.concatenate([mids, new[...]], axis=0), NT_DIMS, preferred_element_type=jnp.float32
    )
    gram = jnp.zeros((size, size), jnp.float32)
    for side in (s0[...], s1[...]):
        gram = gram + lax.dot_general(side, side, NT_DIMS, preferred_element_type=jnp.float32)
    both[...] = total + jnp.concatenate([gram, jnp.zeros_like(gram)], axis=1)


def halo_products(acc, r0, r1, tiles, tab, halo, sums, slots, r2=None):
    edge = GHOST * TB
    halo[:, :edge] = r0[...]
    halo[:, edge : 2 * edge] = r1[...]
    if r2 is not None:

        @pl.when(tab[MISC, 3] == 1)
        def _():
            halo[:, edge : 2 * edge] = r2[...]

    halo[:, 2 * edge :] = jnp.zeros_like(halo[:, 2 * edge :])

    first = (tab[MISC, 0], tab[MISC, 1])

    def term(k, pair):
        row = first[k // GHOST] + k % GHOST
        lhs = jnp.concatenate(
            [block_at(halo, tab[BLOCK + 2 * pair, row]), block_at(halo, tab[BLOCK + 2 * pair + 1, row])], axis=1
        )
        rhs = jnp.concatenate(
            [tiles[row, pl.ds(pl.multiple_of(tab[SLOT + 2 * pair + e, row], TB), TB), :] for e in (0, 1)], axis=0
        )
        return lax.dot_general(lhs, rhs, NN_DIMS, preferred_element_type=jnp.float32)

    for half in (0, GHOST):
        terms = [term(half + u, 0) for u in range(GHOST)]
        for u in range(GHOST):
            at = slice((half + u) * TB, (half + u + 1) * TB)
            sums[:, at] = acc[:, at] + terms[u]
    for g in range(2 * GHOST // SMALL):
        start = first[g * SMALL // GHOST] + g * SMALL % GHOST
        need = tab[NEED, start]
        for u in range(1, SMALL):
            need = jnp.maximum(need, tab[NEED, start + u])

        def more(pair, carry, g=g):
            terms = [term(g * SMALL + u, pair) for u in range(SMALL)]
            for u in range(SMALL):
                at = slice((g * SMALL + u) * TB, (g * SMALL + u + 1) * TB)
                sums[:, at] += terms[u]
            return carry

        lax.fori_loop(1, lax.div(need + 1, 2), more, 0)


def halo_kernel(acc, old0, old1, r0, r1, tiles, tab, *rest, cheb, slots):
    *again, s1, s0, halo, sums = rest
    edge = GHOST * TB
    halo_products(acc, r0, r1, tiles, tab, halo, sums, slots)
    for side, old, new in ((0, old0, s0), (1, old1, s1)):
        value = sums[:, side * edge : (side + 1) * edge]
        if cheb:
            value = 2.0 * value - old[...].astype(jnp.float32)
        new[...] = value.astype(jnp.bfloat16)
    for s2 in again:
        s2[...] = s1[...]


def halo_last_kernel(acc, s0, s1, r0, r1, r2, tiles, tab, both, keep, give, whole, halo, sums, *, slots):
    edge = GHOST * TB
    size = both.shape[0]
    halo_products(acc, r0, r1, tiles, tab, halo, sums, slots, r2)
    cross = both[:, size:]
    for side, y in ((0, s0), (1, s1)):
        image = sums[:, side * edge : (side + 1) * edge].astype(jnp.bfloat16)
        cross = cross + lax.dot_general(y[...], image, NT_DIMS, preferred_element_type=jnp.float32)
    whole[...] = jnp.concatenate([both[:, :size], cross], axis=1)
    half = size // 2
    mine = pl.multiple_of(tab[MISC, 2] * half, half)
    keep[...] = whole[pl.ds(mine, half), :]
    give[...] = whole[pl.ds(pl.multiple_of(half - mine, half), half), :]


def eliminate(gram):
    size = gram.shape[0]
    step, sub = 8, 8
    lanes = lax.broadcasted_iota(jnp.int32, (sub, 2 * size), 1)
    inner = lax.broadcasted_iota(jnp.int32, (sub, 2 * size), 0)
    wide = jnp.concatenate([gram, jnp.zeros_like(gram)], axis=1)
    work = [
        jnp.where(lanes == inner + g * sub + size, 1.0, wide[g * sub : (g + 1) * sub]) for g in range(size // sub)
    ]
    for k in range(0, size, step):
        g0, off = divmod(k, sub)
        cols = [
            {g: jnp.broadcast_to(work[g][:, k + j : k + j + 1], (sub, 2 * size)) for g in range(g0, size // sub)}
            for j in range(step)
        ]
        rows = [work[g0][off + j : off + j + 1] for j in range(step)]
        units = []
        finals = []
        for j in range(step):
            pivot = cols[j][g0][off + j : off + j + 1]
            inverse = 1.0 / pivot
            unit = rows[j] * inverse
            units.append(unit)
            finals.append(rows[j] * lax.rsqrt(pivot))
            for m in range(j + 1, step):
                rows[m] = rows[m] - cols[j][g0][off + m : off + m + 1] * unit
                factor = cols[m][g0][off + j : off + j + 1] * inverse
                cols[m] = {g: cols[m][g] - cols[j][g] * factor for g in cols[m]}
        for g in range(g0, size // sub):
            value = work[g]
            for j in range(step):
                value = value - cols[j][g] * units[j]
            if g == g0:
                value = jnp.where(inner >= off + step, value, work[g])
                for j in range(step):
                    value = jnp.where(inner == off + j, finals[j], value)
            work[g] = value
    return jnp.concatenate(work, axis=0)[:, size:]


def split3(x):
    hi = x.astype(jnp.bfloat16)
    rest = x - hi.astype(jnp.float32)
    mid = rest.astype(jnp.bfloat16)
    low = (rest - mid.astype(jnp.float32)).astype(jnp.bfloat16)
    return hi, mid, low


def end_kernel(mine, other, s0, mid, s1, tab, basis, projected, both, *, nodes_all):
    size = both.shape[0]
    half = size // 2
    at = pl.multiple_of(tab[MISC, 2] * half, half)
    both[pl.ds(at, half), :] = mine[...]
    both[pl.ds(pl.multiple_of(half - at, half), half), :] = other[...]
    edge, inner = s0.shape[1], mid.shape[1]
    values = both[...] / nodes_all
    inverse = eliminate(values[:, :size])
    cross = values[:, size:]
    parts = jnp.concatenate(split3(inverse), axis=0)

    def piece(y):
        out = jnp.dot(parts, y, preferred_element_type=jnp.float32)
        return (out[:size] + (out[size : 2 * size] + out[2 * size :])).astype(jnp.bfloat16)

    lead = pl.multiple_of(tab[MISC, 0] * TB, TB)
    trail = pl.multiple_of(tab[MISC, 1] * TB, TB)
    basis[:, pl.ds(lead, edge)] = piece(s0[...])
    basis[:, pl.ds(trail, edge)] = piece(s1[...])
    for c in range(0, inner, edge):
        basis[:, edge + c : 2 * edge + c] = piece(mid[:, c : c + edge])
    half = jnp.dot(inverse, cross, precision=lax.Precision.HIGHEST, preferred_element_type=jnp.float32)
    projected[...] = lax.dot_general(
        half, inverse, NT_DIMS, precision=lax.Precision.HIGHEST, preferred_element_type=jnp.float32
    )


def rotations(shape, axis):
    at = np.arange(int(np.prod(shape))).reshape(shape)
    return [
        list(zip(at.reshape(-1).tolist(), np.roll(at, -k, axis=axis).reshape(-1).tolist()))
        for k in range(1, shape[axis])
    ]


def all_sum(keep, give, dom, board):
    shape = (dom // 8, 4, 2, board)
    (swap,) = rotations(shape, 2)
    x = keep + lax.ppermute(give, AX, swap)
    planes = np.arange(dom * board).reshape(-1, 2 * board).T.tolist()
    spread = jnp.broadcast_to(x[None], (dom // 2,) + x.shape)
    x = lax.all_to_all(spread, AX, 0, 0, axis_index_groups=planes).sum(0)
    spread = jnp.broadcast_to(x[None], (board,) + x.shape)
    x = lax.all_to_all(spread, "board", 0, 0).sum(0)
    return x, lax.ppermute(x, AX, swap)


def body(block, tiles, cols, counts, *, dom, board):
    devices = dom * board
    size, wide = block.shape
    rows, slots = cols.shape
    edge = GHOST * TB
    inner = wide - 2 * edge
    bf16, f32 = jnp.bfloat16, jnp.float32
    shape = jax.ShapeDtypeStruct
    me = lax.axis_index(AX)
    odd = me % 2

    even_pairs = [(i, i ^ 1) for i in range(devices)]
    odd_pairs = [(i, (((i + 1) ^ 1) - 1) % devices) for i in range(devices)]
    turn = 8 * board
    last_pairs = dict(odd_pairs)
    last_pairs.update({0: turn, turn: 0, turn - 1: devices - 1, devices - 1: turn - 1})
    last_pairs = sorted(last_pairs.items())
    third_pairs = {i: i ^ board for i in range(devices)}
    third_pairs.update({turn - 1: turn, turn: turn - 1})
    for alone, beside in (((turn - 1) ^ board, -1), (turn ^ board, 1)):
        one = alone + beside
        third_pairs.update({one: one ^ board, one ^ board: alone, alone: one})
    third_pairs = sorted(third_pairs.items())

    def exchange(s0, s1, odd_pairs=odd_pairs):
        r1 = lax.ppermute(s1, AX, odd_pairs)
        r0 = lax.ppermute(s0, AX, even_pairs)
        return r0, r1

    head, tail = block[:, :edge], block[:, wide - edge :]
    s0, s1 = jnp.where(odd == 1, head, tail), jnp.where(odd == 1, tail, head)
    r0, r1 = exchange(s0, s1)

    own_flops = 2 * rows * slots * size * TB * TB
    halo_flops = own_flops // 8
    acc_shape = shape((size, 2 * edge), f32)
    mid_shape = shape((size, inner), bf16)
    edge_shape = shape((size, edge), bf16)
    field = pltpu.VMEM((size, wide + TB), bf16)
    halo_scratch = [pltpu.VMEM((size, 2 * edge + TB), bf16), pltpu.VMEM((size, 2 * edge), f32)]

    tiles_v, acc, mid, new, tab = call(
        functools.partial(load_kernel, board=board),
        [shape((rows, slots * TB, TB), bf16), acc_shape, mid_shape, mid_shape, pltpu.SMEM(TABLE, jnp.int32)],
        [VM, VM, HBM, HBM, HBM, HBM],
        [VM, VM, VM, VM, SM],
        [
            field,
            pltpu.VMEM(tiles.shape, bf16),
            pltpu.VMEM((slots, rows), jnp.int32),
            pltpu.VMEM((1, rows), jnp.int32),
            pltpu.VMEM(TABLE, jnp.int32),
            pltpu.SemaphoreType.DMA((rows // GROUP,)),
            pltpu.SemaphoreType.DMA((4,)),
        ],
        limit=40,
        flops=own_flops,
        bytes_=tiles.size * 2,
    )(s0, s1, *(stay(v) for v in (block, tiles, cols.T, counts.reshape(1, rows))))

    tab = pltpu.with_memory_space_constraint(tab, pltpu.SMEM)
    older = (s0, mid, s1)
    for degree in range(DEG):
        old0, old_mid, old1 = older
        older = (s0, mid, s1)
        final = degree == DEG - 1
        *again, s1, s0 = call(
            functools.partial(halo_kernel, cheb=degree > 0, slots=slots),
            [edge_shape] * (3 if final else 2),
            [VM, VM, VM, VM, VM, VM, SM],
            [VM] * (3 if final else 2),
            halo_scratch,
            flops=halo_flops,
        )(acc, old0, old1, r0, r1, tiles_v, tab)
        mid = new
        if final:
            r2 = lax.ppermute(again[0], AX, third_pairs)
        r0, r1 = exchange(s0, s1, last_pairs if final else odd_pairs)
        if degree < DEG - 1:
            acc, new = call(
                functools.partial(own_kernel, slots=slots),
                [acc_shape, mid_shape],
                [VM, VM, VM, VM, VM, SM],
                [VM, VM],
                [field],
                flops=own_flops,
            )(s1, mid, s0, older[1], tiles_v, tab)
        else:
            acc, both = call(
                functools.partial(own_last_kernel, slots=slots),
                [acc_shape, shape((size, 2 * size), f32)],
                [VM, VM, VM, VM, VM, SM],
                [VM, VM],
                [field, pltpu.VMEM((size, inner), bf16)],
                flops=own_flops,
            )(again[0], s1, mid, s0, tiles_v, tab)

    half_shape = shape((size // 2, 2 * size), f32)
    keep, give = call(
        functools.partial(halo_last_kernel, slots=slots),
        [half_shape, half_shape],
        [VM, VM, VM, VM, VM, VM, VM, SM, VM],
        [VM, VM],
        [pltpu.VMEM((size, 2 * size), f32)] + halo_scratch,
        flops=halo_flops,
    )(acc, s0, s1, r0, r1, r2, tiles_v, tab, both)
    mine, other = all_sum(keep, give, dom, board)
    basis, projected = call(
        functools.partial(end_kernel, nodes_all=devices * rows * TB),
        [shape((size, wide), bf16), shape((size, size), f32)],
        [VM, VM, VM, VM, VM, SM],
        [VM, VM],
        [pltpu.VMEM((size, 2 * size), f32)],
        flops=6 * size * size * wide,
    )(mine, other, s0, mid, s1, tab)
    return basis, projected


def solution(mesh):
    dom, board = mesh.shape["dom"], mesh.shape["board"]
    return jax.shard_map(
        functools.partial(body, dom=dom, board=board),
        mesh=mesh,
        in_specs=(
            P(None, AX),
            P(AX, None, None, None),
            P(AX, None),
            P(AX),
        ),
        out_specs=(P(None, AX), P()),
        check_vma=False,
    )
```

```python
import functools

import jax
import jax.numpy as jnp
import numpy as np
from jax import lax
from jax.experimental import pallas as pl
from jax.experimental.pallas import tpu as pltpu
from jax.sharding import PartitionSpec as P

DEG = 4
GHOST = 8
TB = 128
AX = ("dom", "board")
MIB = 1 << 20
NN_DIMS = (((1,), (0,)), ((), ()))
NT_DIMS = (((1,), (1,)), ((), ()))
GROUP = 8
SMALL = 4

VM = pl.BlockSpec(memory_space=pltpu.VMEM)
SM = pl.BlockSpec(memory_space=pltpu.SMEM)
HBM = pl.BlockSpec(memory_space=pltpu.HBM)

OWN, SLOT, BLOCK, NEED, MISC = 0, 10, 20, 30, 31
TABLE = (32, 128)


def call(kernel, out_shape, in_specs, out_specs, scratch=(), limit=24, flops=0, bytes_=0):
    return pl.pallas_call(
        kernel,
        out_shape=out_shape,
        in_specs=in_specs,
        out_specs=out_specs,
        scratch_shapes=scratch,
        compiler_params=pltpu.CompilerParams(vmem_limit_bytes=limit * MIB),
        cost_estimate=pl.CostEstimate(flops=flops, bytes_accessed=bytes_, transcendentals=0),
    )


def stay(x):
    return pltpu.with_memory_space_constraint(x, pltpu.HBM)


def block_at(ref, offset):
    return ref[:, pl.ds(pl.multiple_of(offset, TB), TB)]


def own_row(src, tiles, tab, row, slots):
    total = None
    for pair in range(slots // 2):
        lhs = jnp.concatenate(
            [block_at(src, tab[OWN + 2 * pair, row]), block_at(src, tab[OWN + 2 * pair + 1, row])], axis=1
        )
        rhs = tiles(row, pair)
        term = lax.dot_general(lhs, rhs, NN_DIMS, preferred_element_type=jnp.float32)
        total = term if total is None else total + term
    return total


def gather_field(src, s0, mid, s1):
    edge, inner = s0.shape[1], mid.shape[1]
    src[:, :edge] = s0[...]
    src[:, edge : edge + inner] = mid[...]
    src[:, edge + inner : 2 * edge + inner] = s1[...]
    src[:, 2 * edge + inner :] = jnp.zeros_like(src[:, 2 * edge + inner :])


def own_products(src, pair_of, tab, old, acc, new, cheb, slots, rows, before=None, group=GROUP):
    def place(u, value):
        at = pl.ds(pl.multiple_of(u * TB, TB), TB)
        if cheb:
            value = 2.0 * value - old[:, at].astype(jnp.float32)
        new[:, at] = value.astype(jnp.bfloat16)

    def side(u, value):
        acc[:, pl.ds(pl.multiple_of(u * TB, TB), TB)] = value

    def sweep(first, out, count, store):
        def step(g, carry):
            if before is not None:
                before(first + g * group)
            values = [own_row(src, pair_of, tab, first + g * group + u, slots) for u in range(group)]
            for u in range(group):
                store(out + g * group + u, values[u])
            return carry

        lax.fori_loop(0, count // group, step, 0)

    lead, trail = tab[MISC, 0], tab[MISC, 1]
    sweep(lead, 0, GHOST, side)
    sweep(GHOST, 0, rows - 2 * GHOST, place)
    sweep(trail, GHOST, GHOST, side)


def held_pairs(tiles):
    return lambda row, pair: tiles[row, 2 * pair * TB : 2 * (pair + 1) * TB, :]


def fill_table(cols, counts, place, lines, rows, slots):
    first, odd, core = place[0], place[1], place[2]
    lead = (1 - odd) * (rows - GHOST)
    near = cols[...] - first
    live = lax.broadcasted_iota(jnp.int32, near.shape, 0) < counts[...]
    inside = (near >= 0) & (near < rows)
    spot = jnp.where(near < GHOST, near + lead, jnp.where(near >= rows - GHOST, near - lead, near))
    lines[OWN : OWN + slots, :rows] = jnp.where(live & inside, spot, rows) * TB
    out = jnp.where(live & ~inside, 1, 0)
    there = jnp.where(near < 0, near + GHOST + GHOST * (1 - odd), near - rows + GHOST * odd) * TB
    empty = jnp.zeros((1, rows), jnp.int32)
    found = empty
    slot_lines, block_lines = [empty] * slots, [empty + 2 * GHOST * TB] * slots
    for s in range(slots):
        here = out[s : s + 1]
        for q in range(s + 1):
            hit = (here == 1) & (found == q)
            slot_lines[q] = jnp.where(hit, s * TB, slot_lines[q])
            block_lines[q] = jnp.where(hit, there[s : s + 1], block_lines[q])
        found = found + here
    for q in range(slots):
        lines[SLOT + q : SLOT + q + 1, :rows] = slot_lines[q]
        lines[BLOCK + q : BLOCK + q + 1, :rows] = block_lines[q]
    lines[NEED : NEED + 1, :rows] = found
    lane = lax.broadcasted_iota(jnp.int32, (1, rows), 1)
    lines[MISC : MISC + 1, :rows] = jnp.where(lane == 0, lead, jnp.where(lane == 1, rows - GHOST - lead, jnp.where(lane == 2, core, place[3])))


def load_kernel(
    s0, s1, block, tiles_hbm, cols_hbm, counts_hbm, tiles, acc, mid0, new, tab, src, raw, cols, counts, lines,
    sems, small_sems, *, board,
):
    rows, slots = raw.shape[0], raw.shape[1]
    edge = GHOST * TB
    chunk = GROUP
    me = lax.axis_index(AX)
    turn = 8 * board
    apart = jnp.where((me == turn - 1) | (me == turn), 1, 0)
    place = (me * rows, lax.rem(me, 2), lax.rem(lax.div(me, board), 2), apart)
    little = [
        pltpu.make_async_copy(cols_hbm, cols, small_sems.at[0]),
        pltpu.make_async_copy(counts_hbm, counts, small_sems.at[1]),
        pltpu.make_async_copy(block.at[:, pl.ds(edge, mid0.shape[1])], mid0, small_sems.at[2]),
    ]
    for copy in little:
        copy.start()

    def piece(start):
        return pltpu.make_async_copy(
            tiles_hbm.at[pl.ds(start, chunk)], raw.at[pl.ds(start, chunk)], sems.at[lax.div(start, chunk)]
        )

    lead = (1 - place[1]) * (rows - GHOST)
    for c in range(GHOST // chunk):
        piece(lead + c * chunk).start()
    for c in range(GHOST // chunk, (rows - GHOST) // chunk):
        piece(c * chunk).start()
    for c in range(GHOST // chunk):
        piece(rows - GHOST - lead + c * chunk).start()
    little[0].wait()
    little[1].wait()
    fill_table(cols, counts, place, lines, rows, slots)
    to_scalars = pltpu.make_async_copy(lines, tab, small_sems.at[3])
    to_scalars.start()
    little[2].wait()
    gather_field(src, s0, mid0, s1)
    to_scalars.wait()

    def pair_of(row, pair):
        turned = jnp.concatenate([raw[row, 2 * pair].T, raw[row, 2 * pair + 1].T], axis=0)
        tiles[row, 2 * pair * TB : 2 * (pair + 1) * TB, :] = turned
        return turned

    own_products(
        src, pair_of, tab, None, acc, new, False, slots, rows, before=lambda start: piece(start).wait(), group=chunk
    )


def own_kernel(s1, mid, s0, old, tiles, tab, acc, new, src, *, slots):
    gather_field(src, s0, mid, s1)
    own_products(src, held_pairs(tiles), tab, old, acc, new, True, slots, tiles.shape[0])


def own_last_kernel(s2, s0, mid, s1, tiles, tab, acc, both, src, new, *, slots):
    gather_field(src, s0, mid, s1)
    own_products(src, held_pairs(tiles), tab, None, acc, new, False, slots, tiles.shape[0])
    edge, inner = s0.shape[1], mid.shape[1]
    size = mid.shape[0]
    mids = mid[...]
    total = lax.dot_general(
        mids, jnp.concatenate([mids, new[...]], axis=0), NT_DIMS, preferred_element_type=jnp.float32
    )
    gram = jnp.zeros((size, size), jnp.float32)
    for side in (s0[...], s1[...]):
        gram = gram + lax.dot_general(side, side, NT_DIMS, preferred_element_type=jnp.float32)
    both[...] = total + jnp.concatenate([gram, jnp.zeros_like(gram)], axis=1)


def halo_products(acc, r0, r1, tiles, tab, halo, sums, slots, r2=None):
    edge = GHOST * TB
    halo[:, :edge] = r0[...]
    halo[:, edge : 2 * edge] = r1[...]
    if r2 is not None:

        @pl.when(tab[MISC, 3] == 1)
        def _():
            halo[:, edge : 2 * edge] = r2[...]

    halo[:, 2 * edge :] = jnp.zeros_like(halo[:, 2 * edge :])

    first = (tab[MISC, 0], tab[MISC, 1])

    def term(k, pair):
        row = first[k // GHOST] + k % GHOST
        lhs = jnp.concatenate(
            [block_at(halo, tab[BLOCK + 2 * pair, row]), block_at(halo, tab[BLOCK + 2 * pair + 1, row])], axis=1
        )
        rhs = jnp.concatenate(
            [tiles[row, pl.ds(pl.multiple_of(tab[SLOT + 2 * pair + e, row], TB), TB), :] for e in (0, 1)], axis=0
        )
        return lax.dot_general(lhs, rhs, NN_DIMS, preferred_element_type=jnp.float32)

    for half in (0, GHOST):
        terms = [term(half + u, 0) for u in range(GHOST)]
        for u in range(GHOST):
            at = slice((half + u) * TB, (half + u + 1) * TB)
            sums[:, at] = acc[:, at] + terms[u]
    for g in range(2 * GHOST // SMALL):
        start = first[g * SMALL // GHOST] + g * SMALL % GHOST
        need = tab[NEED, start]
        for u in range(1, SMALL):
            need = jnp.maximum(need, tab[NEED, start + u])

        def more(pair, carry, g=g):
            terms = [term(g * SMALL + u, pair) for u in range(SMALL)]
            for u in range(SMALL):
                at = slice((g * SMALL + u) * TB, (g * SMALL + u + 1) * TB)
                sums[:, at] += terms[u]
            return carry

        lax.fori_loop(1, lax.div(need + 1, 2), more, 0)


def halo_kernel(acc, old0, old1, r0, r1, tiles, tab, *rest, cheb, slots):
    *again, s1, s0, halo, sums = rest
    if again:
        s0, s1 = s1, s0
    edge = GHOST * TB
    halo_products(acc, r0, r1, tiles, tab, halo, sums, slots)
    for side, old, new in ((0, old0, s0), (1, old1, s1)):
        value = sums[:, side * edge : (side + 1) * edge]
        if cheb:
            value = 2.0 * value - old[...].astype(jnp.float32)
        new[...] = value.astype(jnp.bfloat16)
    for s2 in again:
        s2[...] = s1[...]


def halo_last_kernel(acc, s0, s1, r0, r1, r2, tiles, tab, both, keep, give, whole, halo, sums, *, slots):
    edge = GHOST * TB
    size = both.shape[0]
    halo_products(acc, r0, r1, tiles, tab, halo, sums, slots, r2)
    cross = both[:, size:]
    for side, y in ((0, s0), (1, s1)):
        image = sums[:, side * edge : (side + 1) * edge].astype(jnp.bfloat16)
        cross = cross + lax.dot_general(y[...], image, NT_DIMS, preferred_element_type=jnp.float32)
    whole[...] = jnp.concatenate([both[:, :size], cross], axis=1)
    half = size // 2
    mine = pl.multiple_of(tab[MISC, 2] * half, half)
    keep[...] = whole[pl.ds(mine, half), :]
    give[...] = whole[pl.ds(pl.multiple_of(half - mine, half), half), :]


def eliminate(gram):
    size = gram.shape[0]
    step, sub = 8, 8
    lanes = lax.broadcasted_iota(jnp.int32, (sub, 2 * size), 1)
    inner = lax.broadcasted_iota(jnp.int32, (sub, 2 * size), 0)
    wide = jnp.concatenate([gram, jnp.zeros_like(gram)], axis=1)
    work = [
        jnp.where(lanes == inner + g * sub + size, 1.0, wide[g * sub : (g + 1) * sub]) for g in range(size // sub)
    ]
    for k in range(0, size, step):
        g0, off = divmod(k, sub)
        cols = [
            {g: jnp.broadcast_to(work[g][:, k + j : k + j + 1], (sub, 2 * size)) for g in range(g0, size // sub)}
            for j in range(step)
        ]
        rows = [work[g0][off + j : off + j + 1] for j in range(step)]
        units = []
        finals = []
        for j in range(step):
            pivot = cols[j][g0][off + j : off + j + 1]
            inverse = 1.0 / pivot
            unit = rows[j] * inverse
            units.append(unit)
            finals.append(rows[j] * lax.rsqrt(pivot))
            for m in range(j + 1, step):
                rows[m] = rows[m] - cols[j][g0][off + m : off + m + 1] * unit
                factor = cols[m][g0][off + j : off + j + 1] * inverse
                cols[m] = {g: cols[m][g] - cols[j][g] * factor for g in cols[m]}
        for g in range(g0, size // sub):
            value = work[g]
            for j in range(step):
                value = value - cols[j][g] * units[j]
            if g == g0:
                value = jnp.where(inner >= off + step, value, work[g])
                for j in range(step):
                    value = jnp.where(inner == off + j, finals[j], value)
            work[g] = value
    return jnp.concatenate(work, axis=0)[:, size:]


def split3(x):
    hi = x.astype(jnp.bfloat16)
    rest = x - hi.astype(jnp.float32)
    mid = rest.astype(jnp.bfloat16)
    low = (rest - mid.astype(jnp.float32)).astype(jnp.bfloat16)
    return hi, mid, low


def end_kernel(mine, other, s0, mid, s1, tab, basis, projected, both, *, nodes_all):
    size = both.shape[0]
    half = size // 2
    at = pl.multiple_of(tab[MISC, 2] * half, half)
    both[pl.ds(at, half), :] = mine[...]
    both[pl.ds(pl.multiple_of(half - at, half), half), :] = other[...]
    edge, inner = s0.shape[1], mid.shape[1]
    values = both[...] / nodes_all
    inverse = eliminate(values[:, :size])
    cross = values[:, size:]
    parts = jnp.concatenate(split3(inverse), axis=0)

    def piece(y):
        out = jnp.dot(parts, y, preferred_element_type=jnp.float32)
        return (out[:size] + (out[size : 2 * size] + out[2 * size :])).astype(jnp.bfloat16)

    lead = pl.multiple_of(tab[MISC, 0] * TB, TB)
    trail = pl.multiple_of(tab[MISC, 1] * TB, TB)
    basis[:, pl.ds(lead, edge)] = piece(s0[...])
    basis[:, pl.ds(trail, edge)] = piece(s1[...])
    for c in range(0, inner, edge):
        basis[:, edge + c : 2 * edge + c] = piece(mid[:, c : c + edge])
    half = jnp.dot(inverse, cross, precision=lax.Precision.HIGHEST, preferred_element_type=jnp.float32)
    projected[...] = lax.dot_general(
        half, inverse, NT_DIMS, precision=lax.Precision.HIGHEST, preferred_element_type=jnp.float32
    )


def rotations(shape, axis):
    at = np.arange(int(np.prod(shape))).reshape(shape)
    return [
        list(zip(at.reshape(-1).tolist(), np.roll(at, -k, axis=axis).reshape(-1).tolist()))
        for k in range(1, shape[axis])
    ]


def all_sum(keep, give, dom, board):
    shape = (dom // 8, 4, 2, board)
    (swap,) = rotations(shape, 2)
    x = keep + lax.ppermute(give, AX, swap)
    planes = np.arange(dom * board).reshape(-1, 2 * board).T.tolist()
    spread = jnp.broadcast_to(x[None], (dom // 2,) + x.shape)
    x = lax.all_to_all(spread, AX, 0, 0, axis_index_groups=planes).sum(0)
    spread = jnp.broadcast_to(x[None], (board,) + x.shape)
    x = lax.all_to_all(spread, "board", 0, 0).sum(0)
    return x, lax.ppermute(x, AX, swap)


def body(block, tiles, cols, counts, *, dom, board):
    devices = dom * board
    size, wide = block.shape
    rows, slots = cols.shape
    edge = GHOST * TB
    inner = wide - 2 * edge
    bf16, f32 = jnp.bfloat16, jnp.float32
    shape = jax.ShapeDtypeStruct
    me = lax.axis_index(AX)
    odd = me % 2

    even_pairs = [(i, i ^ 1) for i in range(devices)]
    odd_pairs = [(i, (((i + 1) ^ 1) - 1) % devices) for i in range(devices)]
    turn = 8 * board
    last_pairs = dict(odd_pairs)
    last_pairs.update({0: turn, turn: 0, turn - 1: devices - 1, devices - 1: turn - 1})
    last_pairs = sorted(last_pairs.items())
    third_pairs = {i: i ^ board for i in range(devices)}
    third_pairs.update({turn - 1: turn, turn: turn - 1})
    for alone, beside in (((turn - 1) ^ board, -1), (turn ^ board, 1)):
        one = alone + beside
        third_pairs.update({one: one ^ board, one ^ board: alone, alone: one})
    third_pairs = sorted(third_pairs.items())

    def exchange(s0, s1, odd_pairs=odd_pairs):
        r1 = lax.ppermute(s1, AX, odd_pairs)
        r0 = lax.ppermute(s0, AX, even_pairs)
        return r0, r1

    head, tail = block[:, :edge], block[:, wide - edge :]
    s0, s1 = jnp.where(odd == 1, head, tail), jnp.where(odd == 1, tail, head)
    r0, r1 = exchange(s0, s1)

    own_flops = 2 * rows * slots * size * TB * TB
    halo_flops = own_flops // 8
    acc_shape = shape((size, 2 * edge), f32)
    mid_shape = shape((size, inner), bf16)
    edge_shape = shape((size, edge), bf16)
    field = pltpu.VMEM((size, wide + TB), bf16)
    halo_scratch = [pltpu.VMEM((size, 2 * edge + TB), bf16), pltpu.VMEM((size, 2 * edge), f32)]

    tiles_v, acc, mid, new, tab = call(
        functools.partial(load_kernel, board=board),
        [shape((rows, slots * TB, TB), bf16), acc_shape, mid_shape, mid_shape, pltpu.SMEM(TABLE, jnp.int32)],
        [VM, VM, HBM, HBM, HBM, HBM],
        [VM, VM, VM, VM, SM],
        [
            field,
            pltpu.VMEM(tiles.shape, bf16),
            pltpu.VMEM((slots, rows), jnp.int32),
            pltpu.VMEM((1, rows), jnp.int32),
            pltpu.VMEM(TABLE, jnp.int32),
            pltpu.SemaphoreType.DMA((rows // GROUP,)),
            pltpu.SemaphoreType.DMA((4,)),
        ],
        limit=40,
        flops=own_flops,
        bytes_=tiles.size * 2,
    )(s0, s1, *(stay(v) for v in (block, tiles, cols.T, counts.reshape(1, rows))))

    tab = pltpu.with_memory_space_constraint(tab, pltpu.SMEM)
    older = (s0, mid, s1)
    for degree in range(DEG):
        old0, old_mid, old1 = older
        older = (s0, mid, s1)
        final = degree == DEG - 1
        *again, sa, sb = call(
            functools.partial(halo_kernel, cheb=degree > 0, slots=slots),
            [edge_shape] * (3 if final else 2),
            [VM, VM, VM, VM, VM, VM, SM],
            [VM] * (3 if final else 2),
            halo_scratch,
            flops=halo_flops,
        )(acc, old0, old1, r0, r1, tiles_v, tab)
        s0, s1 = (sa, sb) if final else (sb, sa)
        mid = new
        if final:
            r2 = lax.ppermute(again[0], AX, third_pairs)
        r0, r1 = exchange(s0, s1, last_pairs if final else odd_pairs)
        if degree < DEG - 1:
            acc, new = call(
                functools.partial(own_kernel, slots=slots),
                [acc_shape, mid_shape],
                [VM, VM, VM, VM, VM, SM],
                [VM, VM],
                [field],
                flops=own_flops,
            )(s1, mid, s0, older[1], tiles_v, tab)
        else:
            acc, both = call(
                functools.partial(own_last_kernel, slots=slots),
                [acc_shape, shape((size, 2 * size), f32)],
                [VM, VM, VM, VM, VM, SM],
                [VM, VM],
                [field, pltpu.VMEM((size, inner), bf16)],
                flops=own_flops,
            )(again[0], s0, mid, s1, tiles_v, tab)

    half_shape = shape((size // 2, 2 * size), f32)
    keep, give = call(
        functools.partial(halo_last_kernel, slots=slots),
        [half_shape, half_shape],
        [VM, VM, VM, VM, VM, VM, VM, SM, VM],
        [VM, VM],
        [pltpu.VMEM((size, 2 * size), f32)] + halo_scratch,
        flops=halo_flops,
    )(acc, s0, s1, r0, r1, r2, tiles_v, tab, both)
    mine, other = all_sum(keep, give, dom, board)
    basis, projected = call(
        functools.partial(end_kernel, nodes_all=devices * rows * TB),
        [shape((size, wide), bf16), shape((size, size), f32)],
        [VM, VM, VM, VM, VM, SM],
        [VM, VM],
        [pltpu.VMEM((size, 2 * size), f32)],
        flops=6 * size * size * wide,
    )(mine, other, s0, mid, s1, tab)
    return basis, projected


def solution(mesh):
    dom, board = mesh.shape["dom"], mesh.shape["board"]
    return jax.shard_map(
        functools.partial(body, dom=dom, board=board),
        mesh=mesh,
        in_specs=(
            P(None, AX),
            P(AX, None, None, None),
            P(AX, None),
            P(AX),
        ),
        out_specs=(P(None, AX), P()),
        check_vma=False,
    )
```
